256 devices in a mesh: row: 32 (over z, y), col: 8 (over x, core).
Axes of the slice: x: 4, y: 4, z: 8, core: 2. Of those that a mesh axis runs over, the one named last changes fastest.
Arguments:
- leaf_inverse: bfloat16 [256, 1024, 1024], P(('row', 'col')), as said below
- leaf_rhs: bfloat16 [256, 1024, 512], P(('row', 'col')), may hold values from -6 to 6
- leaf_tiles: bfloat16 [256, 1024, 1024], P(('row', 'col')), may hold values from -0.046875 to 0.046875
- mid_inverse_t: bfloat16 [16, 1024, 1024], P('col', None, 'row'), as said below
- mid_rhs: bfloat16 [16, 1024, 512], P('col', 'row'), may hold values from -6 to 6
- mid_tiles: bfloat16 [16, 1024, 1024], P('col', None, 'row'), may hold values from -0.125 to 0.125
- top_inverse_t: bfloat16 [2, 1024, 1024], P(None, None, 'col'), as said below
- top_rhs: bfloat16 [2, 1024, 512], P(None, 'col'), may hold values from -6 to 6
- tile_lists: int32 [256, 1], P(('row', 'col')), may hold values from 0 to 1
Outputs:
- leaf_solved: bfloat16 [256, 1024, 512], P(('row', 'col'))
- mid_solved: bfloat16 [16, 1024, 512], P('col', 'row')
- top_solved: bfloat16 [2, 1024, 512], P(None, 'col')
The draws below stay inside these ranges and needn't reach their ends.
Inputs may be any that keep to these rules, and one draw needn't show every extreme that they name: Each leaf_inverse[d] is zero above its diagonal and has diagonal entries between 0.75 and 1.25. Each mid_inverse_t[q] is zero below its diagonal and has diagonal entries between 0.75 and 1.25. Each top_inverse_t[b] is zero below its diagonal and has diagonal entries between 0.75 and 1.25.
All inputs are finite; a program needn't handle non-finite values.
Results may differ from the reference program's by a relative error of at most 0.0065.
Values may be sent and summed in bfloat16 or wider, within the bound.
A program may use at most 64 MiB of HBM per device.

```python
import math
import jax
import jax.numpy as jnp
from jax import lax

W = 1024
SRC = 512
NB = 2
LEAVES = 256
MID = 16
TOP = 2
N_ROW = 32
N_COL = 8


def triangle(key, number):
    jitter_key, diagonal_key = jax.random.split(key)
    jitter = jnp.clip(jax.random.normal(jitter_key, (number, W, W), jnp.float32), -4.0, 4.0)
    strict_lower = jnp.tril(jnp.ones((W, W), jnp.float32), -1)
    diagonal = jax.random.uniform(diagonal_key, (number, W), jnp.float32, 0.75, 1.25)
    return jitter * strict_lower * (0.8 / math.sqrt(W)) + diagonal[:, :, None] * jnp.eye(W, dtype=jnp.float32)


def draw_leaf_inverse(key, part):
    return triangle(jax.random.fold_in(key, 11), LEAVES).astype(jnp.bfloat16)


def draw_mid_inverse_t(key, part):
    return jnp.swapaxes(triangle(jax.random.fold_in(key, 12), MID), 1, 2).astype(jnp.bfloat16)


def draw_top_inverse_t(key, part):
    return jnp.swapaxes(triangle(jax.random.fold_in(key, 13), TOP), 1, 2).astype(jnp.bfloat16)


def place_ends(result, rng, least, high):
    spot = [jax.random.randint(jax.random.fold_in(rng, axis), (), 0, length) for axis, length in enumerate(result.shape)]
    main_axis = result.shape.index(max(result.shape))
    next_to = spot[:main_axis] + [(spot[main_axis] + 1) % result.shape[main_axis]] + spot[main_axis + 1:]
    return result.at[tuple(spot)].set(least).at[tuple(next_to)].set(high)


def spiked(drawn, stream_key, source, target, blocks, factor):
    def block_of(axis_at):
        return (jnp.arange(drawn.shape[axis_at]) // (drawn.shape[axis_at] // blocks)).reshape((-1,) + (1,) * (drawn.ndim - 1 - axis_at))

    first = jax.random.permutation(stream_key, blocks)[block_of(target)]
    second = (block_of(target) + blocks // 2) % blocks
    return jnp.where((block_of(source) == first) | (block_of(source) == second), factor * drawn, drawn)


def level_of(rng, dims, cuts, least, high):
    factor_of, own = 1.0, jax.random.fold_in(rng, 6)
    for position, shards_of in cuts:
        steps = jnp.exp(jax.random.uniform(jax.random.fold_in(own, position), (shards_of,), jnp.float32, least / len(cuts), high / len(cuts)))
        factor_of = factor_of * jnp.repeat(steps, dims[position] // shards_of).reshape([-1 if axis == position else 1 for axis in range(len(dims))])
    return factor_of


def scatter_about(rng, dims, width, reach, cuts=(), kind=jnp.bfloat16):
    values = width * jax.random.normal(rng, dims, jnp.float32)
    if cuts:
        values = values * level_of(rng, dims, cuts, -0.22, 0.18)
    return jnp.clip(values, -reach, reach).astype(kind)


def bell_draw_with(stream_key, shape, scale, limit, cuts, heavy, kind=jnp.bfloat16):
    entries = scale * jax.random.normal(stream_key, shape, jnp.float32)
    if cuts:
        entries = entries * level_of(stream_key, shape, cuts, -0.22, 0.18)
    return jnp.clip(spiked(entries, jax.random.fold_in(stream_key, 3), *heavy), -limit, limit).astype(kind)


def setup_inputs(seed: int = 0) -> dict:
    arg_keys = jax.random.split(jax.random.key(seed), 10)
    return {
        "leaf_inverse": draw_leaf_inverse(jax.random.fold_in(arg_keys[9], 71), 0),
        "leaf_rhs": scatter_about(arg_keys[1], (LEAVES, W, SRC), 1.0, 6.0, ((0, 256),)),
        "leaf_tiles": scatter_about(arg_keys[2], (LEAVES, W, W), (W * N_ROW // NB) ** -0.5, 0.046875, ((0, 256),)),
        "mid_inverse_t": draw_mid_inverse_t(jax.random.fold_in(arg_keys[9], 71), 0),
        "mid_rhs": scatter_about(arg_keys[4], (MID, W, SRC), 1.0, 6.0, ((0, 8), (1, 32))),
        "mid_tiles": bell_draw_with(arg_keys[5], (MID, W, W), (W * N_COL) ** -0.5, 0.125, ((0, 8), (2, 32)), (2, 1, 32, 2.75)),
        "top_inverse_t": draw_top_inverse_t(jax.random.fold_in(arg_keys[9], 71), 0),
        "top_rhs": scatter_about(arg_keys[7], (TOP, W, SRC), 1.0, 6.0, ((1, 8),)),
        "tile_lists": place_ends(jax.random.randint(arg_keys[8], (LEAVES, 1), 0, NB), jax.random.fold_in(arg_keys[8], 1), 0, NB - 1).astype(jnp.int32),
    }


def reference(leaf_inverse, leaf_rhs, leaf_tiles, mid_inverse_t, mid_rhs, mid_tiles, top_inverse_t, top_rhs, tile_lists):
    def leaf_sweep(running, leaf_index):
        solved = jnp.dot(leaf_inverse[leaf_index], leaf_rhs[leaf_index], preferred_element_type=jnp.float32).astype(jnp.bfloat16)
        update = jnp.dot(leaf_tiles[leaf_index], solved, preferred_element_type=jnp.float32)
        target = ((leaf_index % N_COL) * NB + tile_lists[leaf_index, 0]).astype(jnp.int32)
        return running.at[target].add(update), solved

    leaf_ids = jnp.arange(LEAVES, dtype=jnp.int32)
    mid_update, leaf_solved = lax.scan(leaf_sweep, jnp.zeros((MID, W, SRC), jnp.float32), leaf_ids)
    mid_resid = (mid_rhs.astype(jnp.float32) - mid_update).astype(jnp.bfloat16)
    mid_solved = jnp.einsum("qjw,qjs->qws", mid_inverse_t.astype(jnp.float32), mid_resid.astype(jnp.float32)).astype(jnp.bfloat16)

    tiles_grid = mid_tiles.reshape(N_COL, NB, W, W).astype(jnp.float32)
    solved_grid = mid_solved.reshape(N_COL, NB, W, SRC).astype(jnp.float32)
    top_update = jnp.einsum("cbij,cbjs->bis", tiles_grid, solved_grid)
    top_resid = (top_rhs.astype(jnp.float32) - top_update).astype(jnp.bfloat16)
    top_solved = jnp.einsum("bjw,bjs->bws", top_inverse_t.astype(jnp.float32), top_resid.astype(jnp.float32)).astype(jnp.bfloat16)
    return leaf_solved, mid_solved, top_solved
```

```python
import functools
import jax
import jax.numpy as jnp
from jax import lax
from jax.experimental import pallas as pl
from jax.experimental.pallas import tpu as pltpu
from jax.sharding import PartitionSpec as P

MESH = pl.DeviceIdType.MESH
NZ, NY, NX, NK = 8, 4, 4, 2
NC = NX * NK
W = 1024
SRC = 512
CH = W // NZ
CS = SRC // NY
RB = 256
LAG = 4
F32 = jnp.float32
BF16 = jnp.bfloat16


def kernel(
    li, rhs, tiles, mi, mr, mt, ti, tr, tl,
    leaf_o, mid_o, top_o,
    liv, rv, tv, xv, usend, yrecv, ssend, srecv, rbuf,
    mig, mtg, mrv, flag, flagr, tiv, trv, ybf,
    pbuf, p32, crecv, qbuf, xrecv, zall, tall, tsend,
    load_sem, own_sem, y_s, y_r, mi_s, mi_r, mt_s, mt_r, mr_s, mr_r, fl_s, fl_r,
    s_s, s_r, r_s, r_r, c_s, c_r, x_s, x_r, z_s, z_r, t_s, t_r, mo_s, mo_r, to_s, to_r,
):
    row = lax.axis_index("row")
    col = lax.axis_index("col")
    z, y = row // NY, row % NY
    x, k = col // NK, col % NK

    def at_y(other):
        return (z * NY + other, col)

    def at_z(other):
        return (other * NY + y, col)

    def at_c(other):
        return (row, other)

    def remote(src, dst, s, r, device):
        return pltpu.make_async_remote_copy(
            src_ref=src, dst_ref=dst, send_sem=s, recv_sem=r, device_id=device, device_id_type=MESH
        )

    y_peers = [(y + d) % NY for d in range(1, NY)]

    rbuf[...] = jnp.zeros_like(rbuf)
    barrier = pltpu.get_barrier_semaphore()
    for other in y_peers:
        pl.semaphore_signal(barrier, inc=1, device_id=at_y(other), device_id_type=MESH)
    for d in range(1, NZ):
        pl.semaphore_signal(barrier, inc=1, device_id=at_z((z + d) % NZ), device_id_type=MESH)
    for d in range(1, NC):
        pl.semaphore_signal(barrier, inc=1, device_id=at_c((col + d) % NC), device_id_type=MESH)

    loads = {}

    def load(name, src, dst):
        copy = pltpu.make_async_copy(src, dst, load_sem.at[len(loads)])
        copy.start()
        loads[name] = copy

    for i in range(W // RB):
        rows = slice(i * RB, (i + 1) * RB)
        load(f"r{i}", rhs.at[0, rows, :], rv.at[rows, :])
        load(f"l{i}", li.at[0, rows, : (i + 1) * RB], liv.at[rows, : (i + 1) * RB])
    for i in range(W // RB):
        rows = slice(i * RB, (i + 1) * RB)
        load(f"t{i}", tiles.at[0, rows, :], tv.at[rows, :])
    own_cols = pl.ds(pl.multiple_of(y * CS, CS), CS)
    own_rows = pl.ds(pl.multiple_of(y * 32, 32), 32)
    load("mi", mi, mig.at[y])
    load("mr", mr.at[:, :, own_cols], mrv.at[:, own_rows, :])
    load("mt", mt, mtg.at[y])
    load("ti", ti, tiv)
    load("tr", tr.at[:, :, own_cols], trv)

    flag[...] = jnp.full(flag.shape, tl[0, 0].astype(F32))

    for i in range(W // RB):
        rows = slice(i * RB, (i + 1) * RB)
        loads[f"r{i}"].wait()
        loads[f"l{i}"].wait()
        xv[rows, :] = jnp.dot(
            liv[rows, : (i + 1) * RB], rv[: (i + 1) * RB, :], preferred_element_type=F32
        ).astype(BF16)
    leaf_copy = pltpu.make_async_copy(xv, leaf_o.at[0], own_sem.at[0])
    leaf_copy.start()

    pl.semaphore_wait(barrier, NY + NZ + NC - 3)

    sends = []

    def start(copy):
        copy.start()
        sends.append(copy)
        return copy

    fl_copies, mr_copies = [], []
    for n, other in enumerate(y_peers):
        fl_copies.append(start(remote(flag, flagr.at[n], fl_s.at[n], fl_r.at[n], at_y(other))))
        cols = pl.ds(pl.multiple_of(other * CS, CS), CS)
        mr_copies.append(
            start(remote(mr.at[:, :, cols], mrv.at[:, own_rows, :], mr_s.at[n], mr_r.at[n], at_y(other)))
        )

    def u_copy(j, n):
        return remote(
            usend.at[j, y_peers[n]], yrecv.at[n, j], y_s.at[n, j], y_r.at[n, j], at_y(y_peers[n])
        )

    for i in range(W // RB):
        rows = slice(i * RB, (i + 1) * RB)
        loads[f"t{i}"].wait()
        update = jnp.dot(tv[rows, :], xv[...], preferred_element_type=F32).astype(BF16)
        for h in range(RB // CH):
            j = i * (RB // CH) + h
            for s in range(NY):
                usend[j, s] = update[h * CH : (h + 1) * CH, s * CS : (s + 1) * CS]
            for n in (1, 0, 2):
                start(u_copy(j, n))

    def mi_copy(n):
        return remote(mi, mig.at[y], mi_s.at[n], mi_r.at[n], at_y(y_peers[n]))

    def mt_copy(n):
        return remote(mt, mtg.at[y], mt_s.at[n], mt_r.at[n], at_y(y_peers[n]))

    def s_copy(j):
        return remote(ssend.at[j], srecv.at[z], s_s.at[j], s_r.at[z], at_z(j))

    def r_copy(other):
        part = rbuf.at[:, pl.ds(pl.multiple_of(z * CH, CH), CH), :]
        return remote(part, part, r_s.at[other], r_r.at[z], at_z(other))

    for copy in fl_copies:
        copy.wait_recv()
    loads["mr"].wait()
    for copy in mr_copies:
        copy.wait_recv()

    def chunk(j):
        parts = [(usend[j, y].astype(F32), flag[0:1, :] > 0.5)]
        for n in range(NY - 1):
            u_copy(j, n).wait_recv()
            parts.append((yrecv[n, j].astype(F32), flagr[n, 0:1, :] > 0.5))
        one = sum(jnp.where(f, u, 0.0) for u, f in parts)
        zero = sum(jnp.where(f, 0.0, u) for u, f in parts)
        ssend[j, 0] = zero.astype(BF16)
        ssend[j, 1] = one.astype(BF16)

        @pl.when(z != j)
        def _():
            s_copy(j).start()

    def reduce_own():
        total = ssend[z].astype(F32)
        for d in range(1, NZ):
            other = (z + d) % NZ
            remote(ssend.at[0], srecv.at[other], s_s.at[0], s_r.at[other], at_z(other)).wait_recv()
            total += srecv[other].astype(F32)
        rbuf[:, pl.ds(pl.multiple_of(z * CH, CH), CH), :] = (mrv[...].astype(F32) - total).astype(BF16)
        for other in range(1, NZ):

            @pl.when(other > z)
            def _():
                r_copy(other).start()

    def step(j, carry):
        @pl.when(j < NZ)
        def _():
            chunk(j)

        @pl.when(j == 2)
        def _():
            for n in range(NY - 1):
                mi_copy(n).start()

        @pl.when(j == 5)
        def _():
            for n in range(NY - 1):
                mt_copy(n).start()

        @pl.when(z == j - LAG)
        def _():
            reduce_own()

        return carry

    lax.fori_loop(0, NZ + LAG, step, 0)

    loads["mi"].wait()
    for n in range(NY - 1):
        mi_copy(n).wait_recv()
    for other in range(NZ - 1):

        @pl.when(other < z)
        def _():
            part = rbuf.at[:, other * CH : (other + 1) * CH, :]
            remote(part, part, r_s.at[other], r_r.at[other], at_z(other)).wait_recv()

    turned = []
    for b in range(2):
        solved = jnp.dot(mig[:, b].reshape(CH, W), rbuf[b], preferred_element_type=F32)
        ybf[b] = solved.astype(BF16)
        turned.append(solved.T.astype(BF16))

    loads["mt"].wait()
    for n in range(NY - 1):
        mt_copy(n).wait_recv()
    for b in range(2):
        update = jnp.dot(turned[b], mtg[:, b].reshape(CH, W), preferred_element_type=F32)
        for c in range(NC):
            piece = update[:, c * CH : (c + 1) * CH]
            pbuf[c % NK, c // NK, b] = piece.astype(BF16)
            p32[c % NK, c // NK, b] = piece
    core_copy = start(
        remote(pbuf.at[1 - k], crecv, c_s.at[0], c_r.at[0], at_c(x * NK + 1 - k))
    )

    mid_copies = []
    for n, other in enumerate(y_peers):
        rows = pl.ds(pl.multiple_of(other * 32, 32), 32)
        mid_copies.append(
            start(remote(ybf.at[:, rows, :], mid_o.at[:, :, own_cols], mo_s.at[n], mo_r.at[n], at_y(other)))
        )
    mid_copy = pltpu.make_async_copy(ybf.at[:, own_rows, :], mid_o.at[:, :, own_cols], own_sem.at[1])
    mid_copy.start()

    loads["tr"].wait()
    rhs_t = [trv[b].astype(F32).T for b in range(2)]

    core_copy.wait_recv()
    x_copies = []
    for n in range(NX - 1):
        other = (x + n + 1) % NX
        qbuf[n] = (p32[k, other] + crecv[other].astype(F32)).astype(BF16)
        x_copies.append(
            start(remote(qbuf.at[n], xrecv.at[n], x_s.at[n], x_r.at[n], at_c(other * NK + k)))
        )
    total = p32[k, x] + crecv[x].astype(F32)
    for n in range(NX - 1):
        x_copies[n].wait_recv()
        total += xrecv[n].astype(F32)
    zall[z] = total.astype(BF16)
    for d in range(1, NZ):
        other = (z + d) % NZ
        start(remote(zall.at[z], zall.at[z], z_s.at[d - 1], z_r.at[z], at_z(other)))
    for d in range(1, NZ):
        other = (z + d) % NZ
        remote(zall.at[other], zall.at[other], z_s.at[d - 1], z_r.at[other], at_z(other)).wait_recv()

    mine = pl.ds(pl.multiple_of(col * CH, CH), CH)
    for b in range(2):
        total = zall[0, b].astype(F32)
        for d in range(1, NZ):
            total += zall[d, b].astype(F32)
        tall[b, :, mine] = (rhs_t[b] - total).astype(BF16)
    for d in range(1, NC):
        other = (col + d) % NC
        part = tall.at[:, :, mine]
        start(remote(part, part, t_s.at[d - 1], t_r.at[col], at_c(other)))
    loads["ti"].wait()
    for d in range(1, NC):
        other = (col + d) % NC
        part = tall.at[:, :, pl.ds(pl.multiple_of(other * CH, CH), CH)]
        remote(part, part, t_s.at[d - 1], t_r.at[other], at_c(other)).wait_recv()

    for b in range(2):
        solved = jnp.dot(tall[b], tiv[b], preferred_element_type=F32)
        tsend[b] = solved.T.astype(BF16)
    top_copies = []
    for n, other in enumerate(y_peers):
        top_copies.append(
            start(remote(tsend, top_o.at[:, :, own_cols], to_s.at[n], to_r.at[n], at_y(other)))
        )
    top_copy = pltpu.make_async_copy(tsend, top_o.at[:, :, own_cols], own_sem.at[2])
    top_copy.start()

    leaf_copy.wait()
    mid_copy.wait()
    for n in range(NY - 1):
        mi_copy(n).wait_send()
        mt_copy(n).wait_send()
        mid_copies[n].wait_recv()
    for j in range(NZ):

        @pl.when(z != j)
        def _():
            s_copy(j).wait_send()

        @pl.when(j > z)
        def _():
            r_copy(j).wait_send()

    for copy in sends:
        copy.wait_send()
    top_copy.wait()
    for copy in top_copies:
        copy.wait_recv()


def local(li, rhs, tiles, mi, mr, mt, ti, tr, tl):
    dma = pltpu.SemaphoreType.DMA
    vmem = pltpu.VMEM
    any_spec = pl.BlockSpec(memory_space=pl.ANY)
    n = NY - 1
    return pl.pallas_call(
        kernel,
        out_shape=(
            jax.ShapeDtypeStruct((1, W, SRC), BF16),
            jax.ShapeDtypeStruct((2, 32, SRC), BF16),
            jax.ShapeDtypeStruct((2, CH, SRC), BF16),
        ),
        in_specs=[pl.BlockSpec(memory_space=pltpu.HBM)] * 8 + [pl.BlockSpec(memory_space=pltpu.SMEM)],
        out_specs=(any_spec,) * 3,
        scratch_shapes=[
            vmem((W, W), BF16),
            vmem((W, SRC), BF16),
            vmem((W, W), BF16),
            vmem((W, SRC), BF16),
            vmem((NZ, NY, CH, CS), BF16),
            vmem((n, NZ, CH, CS), BF16),
            vmem((NZ, 2, CH, CS), BF16),
            vmem((NZ, 2, CH, CS), BF16),
            vmem((2, W, CS), BF16),
            vmem((NY, 2, 32, W), BF16),
            vmem((NY, 2, 32, W), BF16),
            vmem((2, CH, CS), BF16),
            vmem((8, 128), F32),
            vmem((n, 8, 128), F32),
            vmem((2, W, CH), BF16),
            vmem((2, CH, CS), BF16),
            vmem((2, CH, CS), BF16),
            vmem((NK, NX, 2, CS, CH), BF16),
            vmem((NK, NX, 2, CS, CH), F32),
            vmem((NX, 2, CS, CH), BF16),
            vmem((NX - 1, 2, CS, CH), BF16),
            vmem((NX - 1, 2, CS, CH), BF16),
            vmem((NZ, 2, CS, CH), BF16),
            vmem((2, CS, W), BF16),
            vmem((2, CH, CS), BF16),
            dma((17,)), dma((3,)),
            dma((n, NZ)), dma((n, NZ)),
            dma((n,)), dma((n,)), dma((n,)), dma((n,)),
            dma((n,)), dma((n,)), dma((n,)), dma((n,)),
            dma((NZ,)), dma((NZ,)), dma((NZ,)), dma((NZ,)),
            dma((1,)), dma((1,)), dma((NX - 1,)), dma((NX - 1,)),
            dma((NZ - 1,)), dma((NZ,)), dma((NC - 1,)), dma((NC,)),
            dma((n,)), dma((n,)), dma((n,)), dma((n,)),
        ],
        compiler_params=pltpu.CompilerParams(
            collective_id=0, has_side_effects=True, vmem_limit_bytes=56 * 1024 * 1024
        ),
        cost_estimate=pl.CostEstimate(flops=2_700_000_000, bytes_accessed=8_000_000, transcendentals=0),
        name="forward_substitution",
    )(li, rhs, tiles, jnp.swapaxes(mi, 1, 2), mr, jnp.swapaxes(mt, 1, 2), ti, tr, tl)


def solution(mesh):
    placed = (
        P(("row", "col"), None, None),
        P(("row", "col"), None, None),
        P(("row", "col"), None, None),
        P("col", None, "row"),
        P("col", "row", None),
        P("col", None, "row"),
        P(None, None, "col"),
        P(None, "col", None),
        P(("row", "col"), None),
    )
    return jax.shard_map(
        local,
        mesh=mesh,
        in_specs=placed,
        out_specs=(P(("row", "col"), None, None), P("col", "row", None), P(None, "col", None)),
        check_vma=False,
    )
```

```python
import functools
import jax
import jax.numpy as jnp
from jax import lax
from jax.experimental import pallas as pl
from jax.experimental.pallas import tpu as pltpu
from jax.sharding import PartitionSpec as P

MESH = pl.DeviceIdType.MESH
NZ, NY, NX, NK = 8, 4, 4, 2
NC = NX * NK
W = 1024
SRC = 512
CH = W // NZ
CS = SRC // NY
CZ = CS // NZ
RB = 256
AHEAD = 3
ORDER = (4, 3, 5, 2, 6, 1, 7, 0)
F32 = jnp.float32
BF16 = jnp.bfloat16


def kernel(
    li, rhs, tiles, mi, mr, mt, ti, tr, tl,
    leaf_o, mid_o, top_o,
    liv, rv, tv, xv, usend, yrecv, up, down, rup, rdown, rbuf,
    mig, mtg, mrv, flag, flagr, tiv, trv, ybf,
    pbuf, p32, crecv, qbuf, xrecv, zsend, zrecv, trt, tall, fall, tsend, midb, topb,
    load_sem, own_sem, y_s, y_r, mi_s, mi_r, mt_s, mt_r, mr_s, mr_r, fl_s, fl_r,
    up_s, up_r, dn_s, dn_r, r_s, f_s, r_r, c_s, c_r, x_s, x_r, z_s, z_r, t_s, t_r, a_s, a_r, mo_s, mo_r, to_s, to_r,
):
    row = lax.axis_index("row")
    col = lax.axis_index("col")
    z, y = row // NY, row % NY
    x, k = col // NK, col % NK

    def at_y(other):
        return (z * NY + other, col)

    def at_z(other):
        return (other * NY + y, col)

    def at_c(other):
        return (row, other)

    def remote(src, dst, s, r, device):
        return pltpu.make_async_remote_copy(
            src_ref=src, dst_ref=dst, send_sem=s, recv_sem=r, device_id=device, device_id_type=MESH
        )

    y_peers = [(y + d) % NY for d in range(1, NY)]

    rbuf[...] = jnp.zeros_like(rbuf)
    barrier = pltpu.get_barrier_semaphore()
    for other in y_peers:
        pl.semaphore_signal(barrier, inc=1, device_id=at_y(other), device_id_type=MESH)
    for d in range(1, NZ):
        pl.semaphore_signal(barrier, inc=1, device_id=at_z((z + d) % NZ), device_id_type=MESH)
    for d in range(1, NC):
        pl.semaphore_signal(barrier, inc=1, device_id=at_c((col + d) % NC), device_id_type=MESH)

    loads = {}

    def load(name, src, dst):
        copy = pltpu.make_async_copy(src, dst, load_sem.at[len(loads)])
        copy.start()
        loads[name] = copy

    for i in range(W // RB):
        rows = slice(i * RB, (i + 1) * RB)
        load(f"r{i}", rhs.at[0, rows, :], rv.at[rows, :])
        load(f"l{i}", li.at[0, rows, : (i + 1) * RB], liv.at[rows, : (i + 1) * RB])
    for i in range(W // RB):
        rows = slice(i * RB, (i + 1) * RB)
        load(f"t{i}", tiles.at[0, rows, :], tv.at[rows, :])
    own_cols = pl.ds(pl.multiple_of(y * CS, CS), CS)
    own_rows = pl.ds(pl.multiple_of(y * 32, 32), 32)
    load("mi", mi, mig.at[y])
    load("mr", mr.at[:, :, own_cols], mrv.at[:, own_rows, :])
    load("mt", mt, mtg.at[y])
    load("ti", ti, tiv)
    load("tr", tr.at[:, :, own_cols], trv)

    flag[...] = jnp.full(flag.shape, tl[0, 0].astype(F32))

    for i in range(W // RB):
        rows = slice(i * RB, (i + 1) * RB)
        loads[f"r{i}"].wait()
        loads[f"l{i}"].wait()
        xv[rows, :] = jnp.dot(
            liv[rows, : (i + 1) * RB], rv[: (i + 1) * RB, :], preferred_element_type=F32
        ).astype(BF16)
    leaf_copy = pltpu.make_async_copy(xv, leaf_o.at[0], own_sem.at[0])
    leaf_copy.start()

    pl.semaphore_wait(barrier, NY + NZ + NC - 3)

    sends = []

    def start(copy):
        copy.start()
        sends.append(copy)
        return copy

    fl_copies, mr_copies = [], []
    for n, other in enumerate(y_peers):
        fl_copies.append(start(remote(flag, flagr.at[n], fl_s.at[n], fl_r.at[n], at_y(other))))
        cols = pl.ds(pl.multiple_of(other * CS, CS), CS)
        mr_copies.append(
            start(remote(mr.at[:, :, cols], mrv.at[:, own_rows, :], mr_s.at[n], mr_r.at[n], at_y(other)))
        )

    def mi_copy(n):
        return remote(mi, mig.at[y], mi_s.at[n], mi_r.at[n], at_y(y_peers[n]))

    def mt_copy(n):
        return remote(mt, mtg.at[y], mt_s.at[n], mt_r.at[n], at_y(y_peers[n]))

    def u_copy(j, n):
        return remote(
            usend.at[j, y_peers[n]], yrecv.at[n, j], y_s.at[n, j], y_r.at[n, j], at_y(y_peers[n])
        )

    for i in range(W // RB):
        loads[f"t{i}"].wait()
    for o in range(NZ):
        chunk_rows = pl.ds(pl.multiple_of((z + ORDER[o]) % NZ * CH, CH), CH)
        update = jnp.dot(tv[chunk_rows, :], xv[...], preferred_element_type=F32).astype(BF16)
        for s in range(NY):
            usend[o, s] = update[:, s * CS : (s + 1) * CS]
        if o < AHEAD:
            for n in (1, 0, 2):
                start(u_copy(o, n))

    above, below = at_z((z + 1) % NZ), at_z((z + NZ - 1) % NZ)

    def up_copy(step):
        part = pl.ds(0, 1 if step == 0 else 2)
        return remote(
            up.at[step, part], rup.at[step, part], up_s.at[step], up_r.at[step], above
        )

    def down_copy(step):
        part = pl.ds(1, 1) if step == 0 else pl.ds(0, 2)
        return remote(
            down.at[step, part], rdown.at[step, part], dn_s.at[step], dn_r.at[step], below
        )

    def r_copy(step):
        part = rbuf.at[:, pl.ds(pl.multiple_of(z * CH, CH), CH), :]
        return remote(part, part, r_s.at[step], r_r.at[z], at_z(z + step))

    def f_copy(step):
        part = rbuf.at[:, pl.ds(pl.multiple_of((z - 2) * CH, CH), CH), :]
        return remote(part, part, f_s.at[step], r_r.at[z - 2], at_z(z + step))

    def r_wait(other):
        part = rbuf.at[:, pl.ds(pl.multiple_of(other * CH, CH), CH), :]
        remote(part, part, r_s.at[0], r_r.at[other], at_z(other)).wait_recv()

    for copy in fl_copies:
        copy.wait_recv()
    loads["mr"].wait()
    for copy in mr_copies:
        copy.wait_recv()

    def summed(o):
        parts = [(usend[o, y].astype(F32), flag[0:1, :] > 0.5)]
        for n in range(NY - 1):
            u_copy(o, n).wait_recv()
            parts.append((yrecv[n, o].astype(F32), flagr[n, 0:1, :] > 0.5))
        if o + AHEAD < NZ:
            for n in (1, 0, 2):
                start(u_copy(o + AHEAD, n))
        one = sum(jnp.where(f, u, 0.0) for u, f in parts)
        zero = sum(jnp.where(f, 0.0, u) for u, f in parts)
        return zero, one

    zero, one = summed(0)
    up[0, 0] = zero.astype(BF16)
    down[0, 1] = one.astype(BF16)
    start(up_copy(0))
    start(down_copy(0))
    for step in range(1, NZ // 2):
        zero, one = summed(2 * step - 1)
        up_copy(step - 1).wait_recv()
        if step > 1:
            one += rup[step - 1, 1].astype(F32)
        up[step, 0] = (zero + rup[step - 1, 0].astype(F32)).astype(BF16)
        up[step, 1] = one.astype(BF16)
        start(up_copy(step))
        zero, one = summed(2 * step)
        down_copy(step - 1).wait_recv()
        if step > 1:
            zero += rdown[step - 1, 0].astype(F32)
        down[step, 0] = zero.astype(BF16)
        down[step, 1] = (one + rdown[step - 1, 1].astype(F32)).astype(BF16)
        start(down_copy(step))
    both = summed(NZ - 1)
    up_copy(NZ // 2 - 1).wait_recv()
    down_copy(NZ // 2 - 1).wait_recv()
    mine = pl.ds(pl.multiple_of(z * CH, CH), CH)
    for b in range(2):
        total = both[b] + rup[NZ // 2 - 1, b].astype(F32) + rdown[NZ // 2 - 1, b].astype(F32)
        rbuf[b, mine, :] = (mrv[b].astype(F32) - total).astype(BF16)
    for step in (2, 1, 7, 6, 5):

        @pl.when(z + step < NZ)
        def _():
            r_copy(step).start()

    for n in (1, 0, 2):
        start(mi_copy(n))
    for n in (1, 0, 2):
        start(mt_copy(n))

    @pl.when(z >= 2)
    def _():
        r_wait(z - 2)
        for step in (2, 1):

            @pl.when(z + step < NZ)
            def _():
                f_copy(step).start()

    loads["mi"].wait()
    for n in range(NY - 1):
        mi_copy(n).wait_recv()
    for other in range(NZ - 1):

        @pl.when((other < z) & (other != z - 2))
        def _():
            r_wait(other)

    turned = []
    for b in range(2):
        solved = jnp.dot(mig[:, b].reshape(CH, W), rbuf[b], preferred_element_type=F32)
        ybf[b] = solved.astype(BF16)
        turned.append(solved.T.astype(BF16))

    loads["mt"].wait()
    for n in range(NY - 1):
        mt_copy(n).wait_recv()
    for b in range(2):
        update = jnp.dot(turned[b], mtg[:, b].reshape(CH, W), preferred_element_type=F32)
        for c in range(NC):
            p32[c % NK, c // NK, b] = update[:, c * CH : (c + 1) * CH]
    pbuf[...] = p32[1 - k].astype(BF16)
    core_copy = start(
        remote(pbuf, crecv, c_s.at[0], c_r.at[0], at_c(x * NK + 1 - k))
    )

    mid_copies = []
    for n, other in enumerate(y_peers):
        rows = pl.ds(pl.multiple_of(other * 32, 32), 32)
        mid_copies.append(start(remote(ybf.at[:, rows, :], midb.at[n], mo_s.at[n], mo_r.at[n], at_y(other))))
    mid_copy = pltpu.make_async_copy(ybf.at[:, own_rows, :], mid_o.at[:, :, own_cols], own_sem.at[1])
    mid_copy.start()

    loads["tr"].wait()
    for b in range(2):
        trt[b] = trv[b].astype(F32).T

    core_copy.wait_recv()
    x_copies = []
    for n in range(NX - 1):
        other = (x + n + 1) % NX
        qbuf[n] = (p32[k, other] + crecv[other].astype(F32)).astype(BF16)
        x_copies.append(
            start(remote(qbuf.at[n], xrecv.at[n], x_s.at[n], x_r.at[n], at_c(other * NK + k)))
        )
    total = p32[k, x] + crecv[x].astype(F32)
    for n in range(NX - 1):
        x_copies[n].wait_recv()
        total += xrecv[n].astype(F32)
    for other in range(NZ):
        zsend[other] = total[:, other * CZ : (other + 1) * CZ, :].astype(BF16)
    my_cols = pl.ds(pl.multiple_of(z * CZ, CZ), CZ)
    for d in range(1, NZ):
        other = (z + d) % NZ
        start(remote(zsend.at[other], zrecv.at[z], z_s.at[d - 1], z_r.at[z], at_z(other)))
    total = zsend[z].astype(F32)
    for d in range(1, NZ):
        other = (z + d) % NZ
        remote(zrecv.at[other], zrecv.at[other], z_s.at[d - 1], z_r.at[other], at_z(other)).wait_recv()
        total += zrecv[other].astype(F32)

    tall[col] = (trt[:, my_cols, :] - total).astype(BF16)
    for d in range(1, NC):
        other = (col + d) % NC
        start(remote(tall.at[col], tall.at[col], t_s.at[d - 1], t_r.at[col], at_c(other)))
    loads["ti"].wait()
    for d in range(1, NC):
        other = (col + d) % NC
        remote(tall.at[other], tall.at[other], t_s.at[d - 1], t_r.at[other], at_c(other)).wait_recv()

    for b in range(2):
        resid = jnp.concatenate([tall[c, b] for c in range(NC)], axis=1)
        fall[z, b] = jnp.dot(resid, tiv[b], preferred_element_type=F32).astype(BF16)
    for d in range(1, NZ):
        other = (z + d) % NZ
        start(remote(fall.at[z], fall.at[z], a_s.at[d - 1], a_r.at[z], at_z(other)))
    for d in range(1, NZ):
        other = (z + d) % NZ
        remote(fall.at[other], fall.at[other], a_s.at[d - 1], a_r.at[other], at_z(other)).wait_recv()
    for b in range(2):
        tsend[b] = fall[:, b].reshape(CS, CH).astype(F32).T.astype(BF16)
    top_copies = []
    for n, other in enumerate(y_peers):
        top_copies.append(start(remote(tsend, topb.at[n], to_s.at[n], to_r.at[n], at_y(other))))
    outs = [leaf_copy, mid_copy]

    def write(src, dst):
        copy = pltpu.make_async_copy(src, dst, own_sem.at[len(outs)])
        copy.start()
        outs.append(copy)

    write(tsend, top_o.at[:, :, own_cols])
    for n in range(NY - 1):
        cols = pl.ds(pl.multiple_of((y + NY - 1 - n) % NY * CS, CS), CS)
        mid_copies[n].wait_recv()
        write(midb.at[n], mid_o.at[:, :, cols])
    for n in (0, 2, 1):
        cols = pl.ds(pl.multiple_of((y + NY - 1 - n) % NY * CS, CS), CS)
        top_copies[n].wait_recv()
        write(topb.at[n], top_o.at[:, :, cols])

    for step in (7, 6, 5, 2, 1):

        @pl.when(z + step < NZ)
        def _():
            r_copy(step).wait_send()

    for step in (2, 1):

        @pl.when((z >= 2) & (z + step < NZ))
        def _():
            f_copy(step).wait_send()

    for copy in sends:
        copy.wait_send()
    for copy in outs:
        copy.wait()


def hand_over(a, b, c, a_o, b_o, c_o, a_v, b_v, c_v, sem):
    rows = W // 4
    moves = [(a.at[0, pl.ds(i * rows, rows)], a_v.at[pl.ds(i * rows, rows)], a_o.at[0, pl.ds(i * rows, rows)]) for i in range(4)]
    moves += [(c, c_v, c_o), (b, b_v, b_o)]
    ins = [pltpu.make_async_copy(src, via, sem.at[0, i]) for i, (src, via, dst) in enumerate(moves)]
    outs = [pltpu.make_async_copy(via, dst, sem.at[1, i]) for i, (src, via, dst) in enumerate(moves)]
    for copy in ins:
        copy.start()
    for i, copy in enumerate(ins):
        copy.wait()
        outs[i].start()
    for copy in outs:
        copy.wait()


def local(li, rhs, tiles, mi, mr, mt, ti, tr, tl):
    dma = pltpu.SemaphoreType.DMA
    vmem = pltpu.VMEM
    any_spec = pl.BlockSpec(memory_space=pl.ANY)
    n = NY - 1
    parts = pl.pallas_call(
        kernel,
        out_shape=(
            jax.ShapeDtypeStruct((1, W, SRC), BF16),
            jax.ShapeDtypeStruct((2, 32, SRC), BF16),
            jax.ShapeDtypeStruct((2, CH, SRC), BF16),
        ),
        in_specs=[pl.BlockSpec(memory_space=pltpu.HBM)] * 8 + [pl.BlockSpec(memory_space=pltpu.SMEM)],
        out_specs=(any_spec,) * 3,
        scratch_shapes=[
            vmem((W, W), BF16),
            vmem((W, SRC), BF16),
            vmem((W, W), BF16),
            vmem((W, SRC), BF16),
            vmem((NZ, NY, CH, CS), BF16),
            vmem((n, NZ, CH, CS), BF16),
            vmem((NZ // 2, 2, CH, CS), BF16),
            vmem((NZ // 2, 2, CH, CS), BF16),
            vmem((NZ // 2, 2, CH, CS), BF16),
            vmem((NZ // 2, 2, CH, CS), BF16),
            vmem((2, W, CS), BF16),
            vmem((NY, 2, 32, W), BF16),
            vmem((NY, 2, 32, W), BF16),
            vmem((2, CH, CS), BF16),
            vmem((8, 128), F32),
            vmem((n, 8, 128), F32),
            vmem((2, W, CH), BF16),
            vmem((2, CH, CS), BF16),
            vmem((2, CH, CS), BF16),
            vmem((NX, 2, CS, CH), BF16),
            vmem((NK, NX, 2, CS, CH), F32),
            vmem((NX, 2, CS, CH), BF16),
            vmem((NX - 1, 2, CS, CH), BF16),
            vmem((NX - 1, 2, CS, CH), BF16),
            vmem((NZ, 2, CZ, CH), BF16),
            vmem((NZ, 2, CZ, CH), BF16),
            vmem((2, CS, CH), F32),
            vmem((NC, 2, CZ, CH), BF16),
            vmem((NZ, 2, CZ, CH), BF16),
            vmem((2, CH, CS), BF16),
            vmem((n, 2, 32, CS), BF16),
            vmem((n, 2, CH, CS), BF16),
            dma((17,)), dma((9,)),
            dma((n, NZ)), dma((n, NZ)),
            dma((n,)), dma((n,)), dma((n,)), dma((n,)),
            dma((n,)), dma((n,)), dma((n,)), dma((n,)),
            dma((NZ // 2,)), dma((NZ // 2,)), dma((NZ // 2,)), dma((NZ // 2,)),
            dma((NZ,)), dma((3,)), dma((NZ,)),
            dma((1,)), dma((1,)), dma((NX - 1,)), dma((NX - 1,)),
            dma((NZ - 1,)), dma((NZ,)), dma((NC - 1,)), dma((NC,)),
            dma((NZ - 1,)), dma((NZ,)),
            dma((n,)), dma((n,)), dma((n,)), dma((n,)),
        ],
        compiler_params=pltpu.CompilerParams(
            collective_id=0, has_side_effects=True, vmem_limit_bytes=56 * 1024 * 1024
        ),
        cost_estimate=pl.CostEstimate(flops=2_700_000_000, bytes_accessed=8_000_000, transcendentals=0),
        name="forward_substitution",
    )(li, rhs, tiles, jnp.swapaxes(mi, 1, 2), mr, jnp.swapaxes(mt, 1, 2), ti, tr, tl)
    return pl.pallas_call(
        hand_over,
        out_shape=tuple(jax.ShapeDtypeStruct(part.shape, part.dtype) for part in parts),
        in_specs=[any_spec] * 3,
        out_specs=(any_spec,) * 3,
        scratch_shapes=[vmem((W, SRC), BF16), vmem((2, 32, SRC), BF16), vmem((2, CH, SRC), BF16), dma((2, 6))],
        name="results",
    )(*parts)


def solution(mesh):
    placed = (
        P(("row", "col"), None, None),
        P(("row", "col"), None, None),
        P(("row", "col"), None, None),
        P("col", None, "row"),
        P("col", "row", None),
        P("col", None, "row"),
        P(None, None, "col"),
        P(None, "col", None),
        P(("row", "col"), None),
    )
    return jax.shard_map(
        local,
        mesh=mesh,
        in_specs=placed,
        out_specs=(P(("row", "col"), None, None), P("col", "row", None), P(None, "col", None)),
        check_vma=False,
    )
```

```python
import functools
import jax
import jax.numpy as jnp
from jax import lax
from jax.experimental import pallas as pl
from jax.experimental.pallas import tpu as pltpu
from jax.sharding import PartitionSpec as P

MESH = pl.DeviceIdType.MESH
NZ, NY, NX, NK = 8, 4, 4, 2
NC = NX * NK
W = 1024
SRC = 512
CH = W // NZ
CS = SRC // NY
CZ = CS // NZ
RB = 256
AHEAD = 3
ORDER = (4, 3, 5, 2, 6, 1, 7, 0)
F32 = jnp.float32
BF16 = jnp.bfloat16


def kernel(
    li, rhs, tiles, mi, mr, mt, ti, tr, tl,
    leaf_o, mid_o, top_o,
    liv, rv, tv, xv, usend, yrecv, up, down, rup, rdown, rbuf,
    mig, mtg, mrv, flag, flagr, tiv, trv, ybf,
    pbuf, p32, crecv, qbuf, xrecv, zsend, zrecv, trt, tall, fall,
    load_sem, own_sem, y_s, y_r, mi_s, mi_r, mt_s, mt_r, mr_s, mr_r, fl_s, fl_r,
    up_s, up_r, dn_s, dn_r, r_s, f_s, r_r, c_s, c_r, x_s, x_r, z_s, z_r, t_s, t_r, a_s, a_r, mo_s, mo_r, to_s, to_r,
):
    row = lax.axis_index("row")
    col = lax.axis_index("col")
    z, y = row // NY, row % NY
    x, k = col // NK, col % NK

    def at_y(other):
        return (z * NY + other, col)

    def at_z(other):
        return (other * NY + y, col)

    def at_c(other):
        return (row, other)

    def remote(src, dst, s, r, device):
        return pltpu.make_async_remote_copy(
            src_ref=src, dst_ref=dst, send_sem=s, recv_sem=r, device_id=device, device_id_type=MESH
        )

    y_peers = [(y + d) % NY for d in range(1, NY)]

    rbuf[...] = jnp.zeros_like(rbuf)
    barrier = pltpu.get_barrier_semaphore()
    for other in y_peers:
        pl.semaphore_signal(barrier, inc=1, device_id=at_y(other), device_id_type=MESH)
    for d in range(1, NZ):
        pl.semaphore_signal(barrier, inc=1, device_id=at_z((z + d) % NZ), device_id_type=MESH)
    for d in range(1, NC):
        pl.semaphore_signal(barrier, inc=1, device_id=at_c((col + d) % NC), device_id_type=MESH)

    loads = {}

    def load(name, src, dst):
        copy = pltpu.make_async_copy(src, dst, load_sem.at[len(loads)])
        copy.start()
        loads[name] = copy

    for i in range(W // RB):
        rows = slice(i * RB, (i + 1) * RB)
        load(f"r{i}", rhs.at[0, rows, :], rv.at[rows, :])
        load(f"l{i}", li.at[0, rows, : (i + 1) * RB], liv.at[rows, : (i + 1) * RB])
    for i in range(W // RB):
        rows = slice(i * RB, (i + 1) * RB)
        load(f"t{i}", tiles.at[0, rows, :], tv.at[rows, :])
    own_cols = pl.ds(pl.multiple_of(y * CS, CS), CS)
    own_rows = pl.ds(pl.multiple_of(y * 32, 32), 32)
    load("mi", mi, mig.at[y])
    load("mr", mr.at[:, :, own_cols], mrv.at[:, own_rows, :])
    load("mt", mt, mtg.at[y])
    load("ti", ti, tiv)
    load("tr", tr.at[:, :, own_cols], trv)

    flag[...] = jnp.full(flag.shape, tl[0, 0].astype(F32))

    for i in range(W // RB):
        rows = slice(i * RB, (i + 1) * RB)
        loads[f"r{i}"].wait()
        loads[f"l{i}"].wait()
        xv[rows, :] = jnp.dot(
            liv[rows, : (i + 1) * RB], rv[: (i + 1) * RB, :], preferred_element_type=F32
        ).astype(BF16)
    leaf_copy = pltpu.make_async_copy(xv, leaf_o.at[0], own_sem.at[0])
    leaf_copy.start()

    pl.semaphore_wait(barrier, NY + NZ + NC - 3)

    sends = []

    def start(copy):
        copy.start()
        sends.append(copy)
        return copy

    fl_copies, mr_copies = [], []
    for n, other in enumerate(y_peers):
        fl_copies.append(start(remote(flag, flagr.at[n], fl_s.at[n], fl_r.at[n], at_y(other))))
        cols = pl.ds(pl.multiple_of(other * CS, CS), CS)
        mr_copies.append(
            start(remote(mr.at[:, :, cols], mrv.at[:, own_rows, :], mr_s.at[n], mr_r.at[n], at_y(other)))
        )

    def mi_copy(n):
        return remote(mi, mig.at[y], mi_s.at[n], mi_r.at[n], at_y(y_peers[n]))

    def mt_copy(n):
        return remote(mt, mtg.at[y], mt_s.at[n], mt_r.at[n], at_y(y_peers[n]))

    def u_copy(j, n):
        return remote(
            usend.at[j, y_peers[n]], yrecv.at[n, j], y_s.at[n, j], y_r.at[n, j], at_y(y_peers[n])
        )

    for i in range(W // RB):
        loads[f"t{i}"].wait()
    for o in range(NZ):
        chunk_rows = pl.ds(pl.multiple_of((z + ORDER[o]) % NZ * CH, CH), CH)
        update = jnp.dot(tv[chunk_rows, :], xv[...], preferred_element_type=F32).astype(BF16)
        for s in range(NY):
            usend[o, s] = update[:, s * CS : (s + 1) * CS]
        if o < AHEAD:
            for n in (1, 0, 2):
                start(u_copy(o, n))

    above, below = at_z((z + 1) % NZ), at_z((z + NZ - 1) % NZ)

    def up_copy(step):
        part = pl.ds(0, 1 if step == 0 else 2)
        return remote(
            up.at[step, part], rup.at[step, part], up_s.at[step], up_r.at[step], above
        )

    def down_copy(step):
        part = pl.ds(1, 1) if step == 0 else pl.ds(0, 2)
        return remote(
            down.at[step, part], rdown.at[step, part], dn_s.at[step], dn_r.at[step], below
        )

    def r_copy(step):
        part = rbuf.at[:, pl.ds(pl.multiple_of(z * CH, CH), CH), :]
        return remote(part, part, r_s.at[step], r_r.at[z], at_z(z + step))

    def f_copy(step):
        part = rbuf.at[:, pl.ds(pl.multiple_of((z - 2) * CH, CH), CH), :]
        return remote(part, part, f_s.at[step], r_r.at[z - 2], at_z(z + step))

    def r_wait(other):
        part = rbuf.at[:, pl.ds(pl.multiple_of(other * CH, CH), CH), :]
        remote(part, part, r_s.at[0], r_r.at[other], at_z(other)).wait_recv()

    for copy in fl_copies:
        copy.wait_recv()
    loads["mr"].wait()
    for copy in mr_copies:
        copy.wait_recv()

    def summed(o):
        parts = [(usend[o, y].astype(F32), flag[0:1, :] > 0.5)]
        for n in range(NY - 1):
            u_copy(o, n).wait_recv()
            parts.append((yrecv[n, o].astype(F32), flagr[n, 0:1, :] > 0.5))
        if o + AHEAD < NZ:
            for n in (1, 0, 2):
                start(u_copy(o + AHEAD, n))
        one = sum(jnp.where(f, u, 0.0) for u, f in parts)
        zero = sum(jnp.where(f, 0.0, u) for u, f in parts)
        return zero, one

    zero, one = summed(0)
    up[0, 0] = zero.astype(BF16)
    down[0, 1] = one.astype(BF16)
    start(up_copy(0))
    start(down_copy(0))
    for step in range(1, NZ // 2):
        zero, one = summed(2 * step - 1)
        up_copy(step - 1).wait_recv()
        if step > 1:
            one += rup[step - 1, 1].astype(F32)
        up[step, 0] = (zero + rup[step - 1, 0].astype(F32)).astype(BF16)
        up[step, 1] = one.astype(BF16)
        start(up_copy(step))
        zero, one = summed(2 * step)
        down_copy(step - 1).wait_recv()
        if step > 1:
            zero += rdown[step - 1, 0].astype(F32)
        down[step, 0] = zero.astype(BF16)
        down[step, 1] = (one + rdown[step - 1, 1].astype(F32)).astype(BF16)
        start(down_copy(step))
    both = summed(NZ - 1)
    up_copy(NZ // 2 - 1).wait_recv()
    down_copy(NZ // 2 - 1).wait_recv()
    mine = pl.ds(pl.multiple_of(z * CH, CH), CH)
    for b in range(2):
        total = both[b] + rup[NZ // 2 - 1, b].astype(F32) + rdown[NZ // 2 - 1, b].astype(F32)
        rbuf[b, mine, :] = (mrv[b].astype(F32) - total).astype(BF16)
    for step in (2, 1, 7, 6, 5):

        @pl.when(z + step < NZ)
        def _():
            r_copy(step).start()

    for n in (1, 0, 2):
        start(mi_copy(n))
    for n in (1, 0, 2):
        start(mt_copy(n))

    @pl.when(z >= 2)
    def _():
        r_wait(z - 2)
        for step in (2, 1):

            @pl.when(z + step < NZ)
            def _():
                f_copy(step).start()

    loads["mi"].wait()
    for n in range(NY - 1):
        mi_copy(n).wait_recv()
    for other in range(NZ - 1):

        @pl.when((other < z) & (other != z - 2))
        def _():
            r_wait(other)

    turned = []
    for b in range(2):
        solved = jnp.dot(mig[:, b].reshape(CH, W), rbuf[b], preferred_element_type=F32)
        ybf[b] = solved.astype(BF16)
        turned.append(solved.T.astype(BF16))

    loads["mt"].wait()
    for n in range(NY - 1):
        mt_copy(n).wait_recv()
    core_copies = []
    for b in range(2):
        update = jnp.dot(turned[b], mtg[:, b].reshape(CH, W), preferred_element_type=F32)
        for c in range(NC):
            p32[c % NK, b, c // NK] = update[:, c * CH : (c + 1) * CH]
        pbuf[b] = p32[1 - k, b].astype(BF16)
        core_copies.append(
            start(remote(pbuf.at[b], crecv.at[b], c_s.at[b], c_r.at[b], at_c(x * NK + 1 - k)))
        )

    mid_copies = []
    for n, other in enumerate(y_peers):
        rows = pl.ds(pl.multiple_of(other * 32, 32), 32)
        mid_copies.append(start(remote(ybf.at[:, rows, :], mid_o.at[y], mo_s.at[n], mo_r.at[n], at_y(other))))
    mid_copy = pltpu.make_async_copy(ybf.at[:, own_rows, :], mid_o.at[y], own_sem.at[1])
    mid_copy.start()

    loads["tr"].wait()
    for b in range(2):
        trt[b] = trv[b].astype(F32).T

    x_copies = []
    sums = []
    for b in range(2):
        core_copies[b].wait_recv()
        for n in range(NX - 1):
            other = (x + n + 1) % NX
            qbuf[b, n] = (p32[k, b, other] + crecv[b, other].astype(F32)).astype(BF16)
            x_copies.append(
                start(
                    remote(qbuf.at[b, n], xrecv.at[b, n], x_s.at[b, n], x_r.at[b, n], at_c(other * NK + k))
                )
            )
        sums.append(p32[k, b, x] + crecv[b, x].astype(F32))
    for b in range(2):
        for n in range(NX - 1):
            x_copies[b * (NX - 1) + n].wait_recv()
            sums[b] += xrecv[b, n].astype(F32)

    for other in range(NZ):
        for b in range(2):
            zsend[other, b] = sums[b][other * CZ : (other + 1) * CZ, :].astype(BF16)
    my_cols = pl.ds(pl.multiple_of(z * CZ, CZ), CZ)
    for d in range(1, NZ):
        other = (z + d) % NZ
        start(remote(zsend.at[other], zrecv.at[z], z_s.at[d - 1], z_r.at[z], at_z(other)))
    total = zsend[z].astype(F32)
    for d in range(1, NZ):
        other = (z + d) % NZ
        remote(zrecv.at[other], zrecv.at[other], z_s.at[d - 1], z_r.at[other], at_z(other)).wait_recv()
        total += zrecv[other].astype(F32)

    tall[col] = (trt[:, my_cols, :] - total).astype(BF16)
    for d in range(1, NC):
        other = (col + d) % NC
        start(remote(tall.at[col], tall.at[col], t_s.at[d - 1], t_r.at[col], at_c(other)))
    loads["ti"].wait()
    for d in range(1, NC):
        other = (col + d) % NC
        remote(tall.at[other], tall.at[other], t_s.at[d - 1], t_r.at[other], at_c(other)).wait_recv()

    for b in range(2):
        resid = jnp.concatenate([tall[c, b] for c in range(NC)], axis=1)
        fall[z, b] = jnp.dot(resid, tiv[b], preferred_element_type=F32).astype(BF16)
    for d in range(1, NZ):
        other = (z + d) % NZ
        start(remote(fall.at[z], fall.at[z], a_s.at[d - 1], a_r.at[z], at_z(other)))
    outs = [leaf_copy, mid_copy]
    to_copies = []

    def pass_on(at, slot):
        for n in (1, 0, 2):
            to_copies.append(
                start(
                    remote(
                        fall.at[at], top_o.at[y, at], to_s.at[n, slot], to_r.at[n, at], at_y(y_peers[n])
                    )
                )
            )
        copy = pltpu.make_async_copy(fall.at[at], top_o.at[y, at], own_sem.at[2 + slot])
        copy.start()
        outs.append(copy)

    pass_on(z, 0)
    for slot, d in enumerate((1, 7, 2, 6, 3, 5, 4)):
        other = (z + d) % NZ
        remote(fall.at[other], fall.at[other], a_s.at[d - 1], a_r.at[other], at_z(other)).wait_recv()
        pass_on(other, slot + 1)

    for step in (7, 6, 5, 2, 1):

        @pl.when(z + step < NZ)
        def _():
            r_copy(step).wait_send()

    for step in (2, 1):

        @pl.when((z >= 2) & (z + step < NZ))
        def _():
            f_copy(step).wait_send()

    for copy in sends:
        copy.wait_send()
    for copy in outs:
        copy.wait()
    for n in range(NY - 1):
        mid_copies[n].wait_recv()
    for copy in to_copies:
        copy.wait_recv()


def hand_over(leaf, mid, top, leaf_o, mid_o, top_o, leaf_v, mid_v, raw_v, top_v, sem):
    rows = W // 4
    parts = [pl.ds(i * rows, rows) for i in range(4)]
    load_top = pltpu.make_async_copy(top, raw_v, sem.at[0, 0])
    load_mid = [
        pltpu.make_async_copy(mid.at[i], mid_v.at[:, :, i * CS : (i + 1) * CS], sem.at[0, 1 + i]) for i in range(NY)
    ]
    load_leaf = [
        pltpu.make_async_copy(leaf.at[0, part], leaf_v.at[part], sem.at[0, 1 + NY + i])
        for i, part in enumerate(parts)
    ]
    stores = [
        pltpu.make_async_copy(leaf_v.at[part], leaf_o.at[0, part], sem.at[1, i]) for i, part in enumerate(parts)
    ]
    store_mid = pltpu.make_async_copy(mid_v, mid_o, sem.at[1, 4])
    store_top = pltpu.make_async_copy(top_v, top_o, sem.at[1, 5])
    for copy in [load_top] + load_leaf + load_mid:
        copy.start()
    load_top.wait()
    for i in range(NY):
        for b in range(2):
            block = raw_v[i, :, b].reshape(CS, CH).astype(F32)
            top_v[b, :, i * CS : (i + 1) * CS] = block.T.astype(BF16)
    store_top.start()
    for load, store in zip(load_leaf, stores):
        load.wait()
        store.start()
    for copy in load_mid:
        copy.wait()
    store_mid.start()
    for copy in stores + [store_mid, store_top]:
        copy.wait()


def local(li, rhs, tiles, mi, mr, mt, ti, tr, tl):
    dma = pltpu.SemaphoreType.DMA
    vmem = pltpu.VMEM
    any_spec = pl.BlockSpec(memory_space=pl.ANY)
    n = NY - 1
    parts = pl.pallas_call(
        kernel,
        out_shape=(
            jax.ShapeDtypeStruct((1, W, SRC), BF16),
            jax.ShapeDtypeStruct((NY, 2, 32, CS), BF16),
            jax.ShapeDtypeStruct((NY, NZ, 2, CZ, CH), BF16),
        ),
        in_specs=[pl.BlockSpec(memory_space=pltpu.HBM)] * 8 + [pl.BlockSpec(memory_space=pltpu.SMEM)],
        out_specs=(any_spec,) * 3,
        scratch_shapes=[
            vmem((W, W), BF16),
            vmem((W, SRC), BF16),
            vmem((W, W), BF16),
            vmem((W, SRC), BF16),
            vmem((NZ, NY, CH, CS), BF16),
            vmem((n, NZ, CH, CS), BF16),
            vmem((NZ // 2, 2, CH, CS), BF16),
            vmem((NZ // 2, 2, CH, CS), BF16),
            vmem((NZ // 2, 2, CH, CS), BF16),
            vmem((NZ // 2, 2, CH, CS), BF16),
            vmem((2, W, CS), BF16),
            vmem((NY, 2, 32, W), BF16),
            vmem((NY, 2, 32, W), BF16),
            vmem((2, CH, CS), BF16),
            vmem((8, 128), F32),
            vmem((n, 8, 128), F32),
            vmem((2, W, CH), BF16),
            vmem((2, CH, CS), BF16),
            vmem((2, CH, CS), BF16),
            vmem((2, NX, CS, CH), BF16),
            vmem((NK, 2, NX, CS, CH), F32),
            vmem((2, NX, CS, CH), BF16),
            vmem((2, NX - 1, CS, CH), BF16),
            vmem((2, NX - 1, CS, CH), BF16),
            vmem((NZ, 2, CZ, CH), BF16),
            vmem((NZ, 2, CZ, CH), BF16),
            vmem((2, CS, CH), F32),
            vmem((NC, 2, CZ, CH), BF16),
            vmem((NZ, 2, CZ, CH), BF16),
            dma((17,)), dma((2 + NZ,)),
            dma((n, NZ)), dma((n, NZ)),
            dma((n,)), dma((n,)), dma((n,)), dma((n,)),
            dma((n,)), dma((n,)), dma((n,)), dma((n,)),
            dma((NZ // 2,)), dma((NZ // 2,)), dma((NZ // 2,)), dma((NZ // 2,)),
            dma((NZ,)), dma((3,)), dma((NZ,)),
            dma((2,)), dma((2,)), dma((2, NX - 1)), dma((2, NX - 1)),
            dma((NZ - 1,)), dma((NZ,)), dma((NC - 1,)), dma((NC,)),
            dma((NZ - 1,)), dma((NZ,)),
            dma((n,)), dma((n,)), dma((n, NZ)), dma((n, NZ)),
        ],
        compiler_params=pltpu.CompilerParams(
            collective_id=0, has_side_effects=True, vmem_limit_bytes=56 * 1024 * 1024
        ),
        cost_estimate=pl.CostEstimate(flops=2_700_000_000, bytes_accessed=8_000_000, transcendentals=0),
        name="forward_substitution",
    )(li, rhs, tiles, jnp.swapaxes(mi, 1, 2), mr, jnp.swapaxes(mt, 1, 2), ti, tr, tl)
    return pl.pallas_call(
        hand_over,
        out_shape=(
            jax.ShapeDtypeStruct((1, W, SRC), BF16),
            jax.ShapeDtypeStruct((2, 32, SRC), BF16),
            jax.ShapeDtypeStruct((2, CH, SRC), BF16),
        ),
        in_specs=[any_spec] * 3,
        out_specs=(any_spec,) * 3,
        scratch_shapes=[
            vmem((W, SRC), BF16),
            vmem((2, 32, SRC), BF16),
            vmem((NY, NZ, 2, CZ, CH), BF16),
            vmem((2, CH, SRC), BF16),
            dma((2, 9)),
        ],
        name="results",
    )(*parts)


def solution(mesh):
    placed = (
        P(("row", "col"), None, None),
        P(("row", "col"), None, None),
        P(("row", "col"), None, None),
        P("col", None, "row"),
        P("col", "row", None),
        P("col", None, "row"),
        P(None, None, "col"),
        P(None, "col", None),
        P(("row", "col"), None),
    )
    return jax.shard_map(
        local,
        mesh=mesh,
        in_specs=placed,
        out_specs=(P(("row", "col"), None, None), P("col", "row", None), P(None, "col", None)),
        check_vma=False,
    )
```

```python
import functools
import jax
import jax.numpy as jnp
from jax import lax
from jax.experimental import pallas as pl
from jax.experimental.pallas import tpu as pltpu
from jax.sharding import PartitionSpec as P

MESH = pl.DeviceIdType.MESH
NZ, NY, NX, NK = 8, 4, 4, 2
NC = NX * NK
W = 1024
SRC = 512
CH = W // NZ
CS = SRC // NY
CZ = CS // NZ
RB = 256
AHEAD = 3
ORDER = (4, 3, 5, 2, 6, 1, 7, 0)
F32 = jnp.float32
BF16 = jnp.bfloat16


def kernel(
    li, rhs, tiles, mi, mr, mt, ti, tr, tl,
    leaf_o, mid_o, top_o,
    liv, rv, tv, xv, usend, yrecv, up, down, rup, rdown, rbuf,
    mig, mtg, mrv, flag, flagr, tiv, trv, ybf,
    pbuf, p32, crecv, qbuf, xrecv, trt, tall, fall,
    load_sem, own_sem, y_s, y_r, mi_s, mi_r, mt_s, mt_r, mr_s, mr_r, fl_s, fl_r,
    up_s, up_r, dn_s, dn_r, r_s, f_s, r_r, c_s, c_r, x_s, x_r, t_s, t_r, a_s, a_r, mo_s, mo_r, to_s, to_r, ring_in,
):
    row = lax.axis_index("row")
    col = lax.axis_index("col")
    z, y = row // NY, row % NY
    x, k = col // NK, col % NK

    def at_y(other):
        return (z * NY + other, col)

    def at_z(other):
        return (other * NY + y, col)

    def at_c(other):
        return (row, other)

    def at_xz(other_x, other_z):
        return (other_z * NY + y, other_x * NK + k)

    def remote(src, dst, s, r, device):
        return pltpu.make_async_remote_copy(
            src_ref=src, dst_ref=dst, send_sem=s, recv_sem=r, device_id=device, device_id_type=MESH
        )

    y_peers = [(y + d) % NY for d in range(1, NY)]

    rbuf[...] = jnp.zeros_like(rbuf)
    barrier = pltpu.get_barrier_semaphore()
    for other in y_peers:
        pl.semaphore_signal(barrier, inc=1, device_id=at_y(other), device_id_type=MESH)
    for d in range(1, NZ):
        pl.semaphore_signal(barrier, inc=1, device_id=at_z((z + d) % NZ), device_id_type=MESH)
    for d in range(1, NC):
        pl.semaphore_signal(barrier, inc=1, device_id=at_c((col + d) % NC), device_id_type=MESH)

    loads = {}

    def load(name, src, dst):
        copy = pltpu.make_async_copy(src, dst, load_sem.at[len(loads)])
        copy.start()
        loads[name] = copy

    for i in range(W // RB):
        rows = slice(i * RB, (i + 1) * RB)
        load(f"r{i}", rhs.at[0, rows, :], rv.at[rows, :])
        load(f"l{i}", li.at[0, rows, : (i + 1) * RB], liv.at[rows, : (i + 1) * RB])
    for i in range(W // RB):
        rows = slice(i * RB, (i + 1) * RB)
        load(f"t{i}", tiles.at[0, rows, :], tv.at[rows, :])
    own_cols = pl.ds(pl.multiple_of(y * CS, CS), CS)
    own_rows = pl.ds(pl.multiple_of(y * 32, 32), 32)
    load("mi", mi, mig.at[y])
    load("mr", mr.at[:, :, own_cols], mrv.at[:, own_rows, :])
    load("mt", mt, mtg.at[y])
    load("ti", ti, tiv)
    load("tr", tr.at[:, :, own_cols], trv)

    flag[...] = jnp.full(flag.shape, tl[0, 0].astype(F32))

    for i in range(W // RB):
        rows = slice(i * RB, (i + 1) * RB)
        loads[f"r{i}"].wait()
        loads[f"l{i}"].wait()
        xv[rows, :] = jnp.dot(
            liv[rows, : (i + 1) * RB], rv[: (i + 1) * RB, :], preferred_element_type=F32
        ).astype(BF16)
    leaf_copy = pltpu.make_async_copy(xv, leaf_o.at[0], own_sem.at[0])
    leaf_copy.start()

    pl.semaphore_wait(barrier, NY + NZ + NC - 3)

    for d in range(1, NX):
        pl.semaphore_signal(ring_in, inc=1, device_id=at_c((x + d) % NX * NK + k), device_id_type=MESH)

    sends = []

    def start(copy):
        copy.start()
        sends.append(copy)
        return copy

    fl_copies, mr_copies = [], []
    for n, other in enumerate(y_peers):
        fl_copies.append(start(remote(flag, flagr.at[n], fl_s.at[n], fl_r.at[n], at_y(other))))
        cols = pl.ds(pl.multiple_of(other * CS, CS), CS)
        mr_copies.append(
            start(remote(mr.at[:, :, cols], mrv.at[:, own_rows, :], mr_s.at[n], mr_r.at[n], at_y(other)))
        )

    def mi_copy(n):
        return remote(mi, mig.at[y], mi_s.at[n], mi_r.at[n], at_y(y_peers[n]))

    def mt_copy(n):
        return remote(mt, mtg.at[y], mt_s.at[n], mt_r.at[n], at_y(y_peers[n]))

    def u_copy(j, n):
        return remote(
            usend.at[j, y_peers[n]], yrecv.at[n, j], y_s.at[n, j], y_r.at[n, j], at_y(y_peers[n])
        )

    for i in range(W // RB):
        loads[f"t{i}"].wait()
    for o in range(NZ):
        chunk_rows = pl.ds(pl.multiple_of((z + ORDER[o]) % NZ * CH, CH), CH)
        update = jnp.dot(tv[chunk_rows, :], xv[...], preferred_element_type=F32).astype(BF16)
        for s in range(NY):
            usend[o, s] = update[:, s * CS : (s + 1) * CS]
        if o < AHEAD:
            for n in (1, 0, 2):
                start(u_copy(o, n))

    above, below = at_z((z + 1) % NZ), at_z((z + NZ - 1) % NZ)

    def up_copy(step):
        part = pl.ds(0, 1 if step == 0 else 2)
        return remote(
            up.at[step, part], rup.at[step, part], up_s.at[step], up_r.at[step], above
        )

    def down_copy(step):
        part = pl.ds(1, 1) if step == 0 else pl.ds(0, 2)
        return remote(
            down.at[step, part], rdown.at[step, part], dn_s.at[step], dn_r.at[step], below
        )

    def r_copy(step):
        part = rbuf.at[:, pl.ds(pl.multiple_of(z * CH, CH), CH), :]
        return remote(part, part, r_s.at[step], r_r.at[z], at_z(z + step))

    def f_copy(step):
        part = rbuf.at[:, pl.ds(pl.multiple_of((z - 2) * CH, CH), CH), :]
        return remote(part, part, f_s.at[step], r_r.at[z - 2], at_z(z + step))

    def r_wait(other):
        part = rbuf.at[:, pl.ds(pl.multiple_of(other * CH, CH), CH), :]
        remote(part, part, r_s.at[0], r_r.at[other], at_z(other)).wait_recv()

    for copy in fl_copies:
        copy.wait_recv()
    loads["mr"].wait()
    for copy in mr_copies:
        copy.wait_recv()

    def summed(o):
        parts = [(usend[o, y].astype(F32), flag[0:1, :] > 0.5)]
        for n in range(NY - 1):
            u_copy(o, n).wait_recv()
            parts.append((yrecv[n, o].astype(F32), flagr[n, 0:1, :] > 0.5))
        if o + AHEAD < NZ:
            for n in (1, 0, 2):
                start(u_copy(o + AHEAD, n))
        one = sum(jnp.where(f, u, 0.0) for u, f in parts)
        zero = sum(jnp.where(f, 0.0, u) for u, f in parts)
        return zero, one

    zero, one = summed(0)
    up[0, 0] = zero.astype(BF16)
    down[0, 1] = one.astype(BF16)
    start(up_copy(0))
    start(down_copy(0))
    for step in range(1, NZ // 2):
        zero, one = summed(2 * step - 1)
        up_copy(step - 1).wait_recv()
        if step > 1:
            one += rup[step - 1, 1].astype(F32)
        up[step, 0] = (zero + rup[step - 1, 0].astype(F32)).astype(BF16)
        up[step, 1] = one.astype(BF16)
        start(up_copy(step))
        zero, one = summed(2 * step)
        down_copy(step - 1).wait_recv()
        if step > 1:
            zero += rdown[step - 1, 0].astype(F32)
        down[step, 0] = zero.astype(BF16)
        down[step, 1] = (one + rdown[step - 1, 1].astype(F32)).astype(BF16)
        start(down_copy(step))
    both = summed(NZ - 1)
    up_copy(NZ // 2 - 1).wait_recv()
    down_copy(NZ // 2 - 1).wait_recv()
    mine = pl.ds(pl.multiple_of(z * CH, CH), CH)
    for b in range(2):
        total = both[b] + rup[NZ // 2 - 1, b].astype(F32) + rdown[NZ // 2 - 1, b].astype(F32)
        rbuf[b, mine, :] = (mrv[b].astype(F32) - total).astype(BF16)
    for step in (2, 1, 7, 6, 5):

        @pl.when(z + step < NZ)
        def _():
            r_copy(step).start()

    for n in (1, 0, 2):
        start(mi_copy(n))
    for n in (1, 0, 2):
        start(mt_copy(n))

    @pl.when(z >= 2)
    def _():
        r_wait(z - 2)
        for step in (2, 1):

            @pl.when(z + step < NZ)
            def _():
                f_copy(step).start()

    loads["mi"].wait()
    for n in range(NY - 1):
        mi_copy(n).wait_recv()
    for other in range(NZ - 1):

        @pl.when((other < z) & (other != z - 2))
        def _():
            r_wait(other)

    turned = []
    for b in range(2):
        solved = jnp.dot(mig[:, b].reshape(CH, W), rbuf[b], preferred_element_type=F32)
        ybf[b] = solved.astype(BF16)
        turned.append(solved.T.astype(BF16))

    loads["mt"].wait()
    for n in range(NY - 1):
        mt_copy(n).wait_recv()
    core_copies = []
    for b in range(2):
        update = jnp.dot(turned[b], mtg[:, b].reshape(CH, W), preferred_element_type=F32)
        for c in range(NC):
            p32[c % NK, b, c // NK] = update[:, c * CH : (c + 1) * CH]
        pbuf[b] = p32[1 - k, b].astype(BF16)
        core_copies.append(
            start(remote(pbuf.at[b], crecv.at[b], c_s.at[b], c_r.at[b], at_c(x * NK + 1 - k)))
        )

    mid_copies = []
    for n, other in enumerate(y_peers):
        rows = pl.ds(pl.multiple_of(other * 32, 32), 32)
        mid_copies.append(start(remote(ybf.at[:, rows, :], mid_o.at[y], mo_s.at[n], mo_r.at[n], at_y(other))))
    mid_copy = pltpu.make_async_copy(ybf.at[:, own_rows, :], mid_o.at[y], own_sem.at[1])
    mid_copy.start()

    loads["tr"].wait()
    for b in range(2):
        trt[b] = trv[b].astype(F32).T

    for b in range(2):
        core_copies[b].wait_recv()
        for other in range(NX):
            part = (p32[k, b, other] + crecv[b, other].astype(F32)).astype(BF16)
            for slot in range(NZ):
                qbuf[other, slot, b] = part[slot * CZ : (slot + 1) * CZ, :]
    steps = [(dx, dz) for dz in (4, 3, 5, 2, 6, 1, 7, 0) for dx in (2, 1, 3, 0) if dx or dz]
    pl.semaphore_wait(ring_in, NX - 1)
    for dx, dz in steps:
        ox, oz = (x + dx) % NX, (z + dz) % NZ
        start(
            remote(qbuf.at[ox, oz], xrecv.at[x, z], x_s.at[dx, dz], x_r.at[x, z], at_xz(ox, oz))
        )
    total = qbuf[x, z].astype(F32)
    for dx, dz in reversed(steps):
        ox, oz = (x + dx) % NX, (z + dz) % NZ
        remote(
            xrecv.at[ox, oz], xrecv.at[ox, oz], x_s.at[dx, dz], x_r.at[ox, oz], at_xz(ox, oz)
        ).wait_recv()
        total += xrecv[ox, oz].astype(F32)
    my_cols = pl.ds(pl.multiple_of(z * CZ, CZ), CZ)

    tall[col] = (trt[:, my_cols, :] - total).astype(BF16)
    for d in range(1, NC):
        other = (col + d) % NC
        start(remote(tall.at[col], tall.at[col], t_s.at[d - 1], t_r.at[col], at_c(other)))
    loads["ti"].wait()
    for d in range(1, NC):
        other = (col + d) % NC
        remote(tall.at[other], tall.at[other], t_s.at[d - 1], t_r.at[other], at_c(other)).wait_recv()

    for b in range(2):
        resid = jnp.concatenate([tall[c, b] for c in range(NC)], axis=1)
        fall[z, b] = jnp.dot(resid, tiv[b], preferred_element_type=F32).astype(BF16)
    for d in range(1, NZ):
        other = (z + d) % NZ
        start(remote(fall.at[z], fall.at[z], a_s.at[d - 1], a_r.at[z], at_z(other)))
    outs = [leaf_copy, mid_copy]
    to_copies = []

    def pass_on(at, slot):
        for n in (1, 0, 2):
            to_copies.append(
                start(
                    remote(
                        fall.at[at], top_o.at[y, at], to_s.at[n, slot], to_r.at[n, at], at_y(y_peers[n])
                    )
                )
            )
        copy = pltpu.make_async_copy(fall.at[at], top_o.at[y, at], own_sem.at[2 + slot])
        copy.start()
        outs.append(copy)

    pass_on(z, 0)
    for slot, d in enumerate((1, 7, 2, 6, 3, 5, 4)):
        other = (z + d) % NZ
        remote(fall.at[other], fall.at[other], a_s.at[d - 1], a_r.at[other], at_z(other)).wait_recv()
        pass_on(other, slot + 1)

    for step in (7, 6, 5, 2, 1):

        @pl.when(z + step < NZ)
        def _():
            r_copy(step).wait_send()

    for step in (2, 1):

        @pl.when((z >= 2) & (z + step < NZ))
        def _():
            f_copy(step).wait_send()

    for copy in sends:
        copy.wait_send()
    for copy in outs:
        copy.wait()
    for n in range(NY - 1):
        mid_copies[n].wait_recv()
    for copy in to_copies:
        copy.wait_recv()


def hand_over(leaf, mid, top, leaf_o, mid_o, top_o, leaf_v, mid_v, raw_v, top_v, sem):
    rows = W // 4
    parts = [pl.ds(i * rows, rows) for i in range(4)]
    load_top = pltpu.make_async_copy(top, raw_v, sem.at[0, 0])
    load_mid = [
        pltpu.make_async_copy(mid.at[i], mid_v.at[:, :, i * CS : (i + 1) * CS], sem.at[0, 1 + i]) for i in range(NY)
    ]
    load_leaf = [
        pltpu.make_async_copy(leaf.at[0, part], leaf_v.at[part], sem.at[0, 1 + NY + i])
        for i, part in enumerate(parts)
    ]
    stores = [
        pltpu.make_async_copy(leaf_v.at[part], leaf_o.at[0, part], sem.at[1, i]) for i, part in enumerate(parts)
    ]
    store_mid = pltpu.make_async_copy(mid_v, mid_o, sem.at[1, 4])
    store_top = pltpu.make_async_copy(top_v, top_o, sem.at[1, 5])
    for copy in [load_top] + load_leaf + load_mid:
        copy.start()
    load_top.wait()
    for i in range(NY):
        for b in range(2):
            block = raw_v[i, :, b].reshape(CS, CH).astype(F32)
            top_v[b, :, i * CS : (i + 1) * CS] = block.T.astype(BF16)
    store_top.start()
    for load, store in zip(load_leaf, stores):
        load.wait()
        store.start()
    for copy in load_mid:
        copy.wait()
    store_mid.start()
    for copy in stores + [store_mid, store_top]:
        copy.wait()


def local(li, rhs, tiles, mi, mr, mt, ti, tr, tl):
    dma = pltpu.SemaphoreType.DMA
    vmem = pltpu.VMEM
    any_spec = pl.BlockSpec(memory_space=pl.ANY)
    n = NY - 1
    parts = pl.pallas_call(
        kernel,
        out_shape=(
            jax.ShapeDtypeStruct((1, W, SRC), BF16),
            jax.ShapeDtypeStruct((NY, 2, 32, CS), BF16),
            jax.ShapeDtypeStruct((NY, NZ, 2, CZ, CH), BF16),
        ),
        in_specs=[pl.BlockSpec(memory_space=pltpu.HBM)] * 8 + [pl.BlockSpec(memory_space=pltpu.SMEM)],
        out_specs=(any_spec,) * 3,
        scratch_shapes=[
            vmem((W, W), BF16),
            vmem((W, SRC), BF16),
            vmem((W, W), BF16),
            vmem((W, SRC), BF16),
            vmem((NZ, NY, CH, CS), BF16),
            vmem((n, NZ, CH, CS), BF16),
            vmem((NZ // 2, 2, CH, CS), BF16),
            vmem((NZ // 2, 2, CH, CS), BF16),
            vmem((NZ // 2, 2, CH, CS), BF16),
            vmem((NZ // 2, 2, CH, CS), BF16),
            vmem((2, W, CS), BF16),
            vmem((NY, 2, 32, W), BF16),
            vmem((NY, 2, 32, W), BF16),
            vmem((2, CH, CS), BF16),
            vmem((8, 128), F32),
            vmem((n, 8, 128), F32),
            vmem((2, W, CH), BF16),
            vmem((2, CH, CS), BF16),
            vmem((2, CH, CS), BF16),
            vmem((2, NX, CS, CH), BF16),
            vmem((NK, 2, NX, CS, CH), F32),
            vmem((2, NX, CS, CH), BF16),
            vmem((NX, NZ, 2, CZ, CH), BF16),
            vmem((NX, NZ, 2, CZ, CH), BF16),
            vmem((2, CS, CH), F32),
            vmem((NC, 2, CZ, CH), BF16),
            vmem((NZ, 2, CZ, CH), BF16),
            dma((17,)), dma((2 + NZ,)),
            dma((n, NZ)), dma((n, NZ)),
            dma((n,)), dma((n,)), dma((n,)), dma((n,)),
            dma((n,)), dma((n,)), dma((n,)), dma((n,)),
            dma((NZ // 2,)), dma((NZ // 2,)), dma((NZ // 2,)), dma((NZ // 2,)),
            dma((NZ,)), dma((3,)), dma((NZ,)),
            dma((2,)), dma((2,)), dma((NX, NZ)), dma((NX, NZ)),
            dma((NC - 1,)), dma((NC,)),
            dma((NZ - 1,)), dma((NZ,)),
            dma((n,)), dma((n,)), dma((n, NZ)), dma((n, NZ)),
            pltpu.SemaphoreType.REGULAR,
        ],
        compiler_params=pltpu.CompilerParams(
            collective_id=0, has_side_effects=True, vmem_limit_bytes=56 * 1024 * 1024
        ),
        cost_estimate=pl.CostEstimate(flops=2_700_000_000, bytes_accessed=8_000_000, transcendentals=0),
        name="forward_substitution",
    )(li, rhs, tiles, jnp.swapaxes(mi, 1, 2), mr, jnp.swapaxes(mt, 1, 2), ti, tr, tl)
    return pl.pallas_call(
        hand_over,
        out_shape=(
            jax.ShapeDtypeStruct((1, W, SRC), BF16),
            jax.ShapeDtypeStruct((2, 32, SRC), BF16),
            jax.ShapeDtypeStruct((2, CH, SRC), BF16),
        ),
        in_specs=[any_spec] * 3,
        out_specs=(any_spec,) * 3,
        scratch_shapes=[
            vmem((W, SRC), BF16),
            vmem((2, 32, SRC), BF16),
            vmem((NY, NZ, 2, CZ, CH), BF16),
            vmem((2, CH, SRC), BF16),
            dma((2, 9)),
        ],
        name="results",
    )(*parts)


def solution(mesh):
    placed = (
        P(("row", "col"), None, None),
        P(("row", "col"), None, None),
        P(("row", "col"), None, None),
        P("col", None, "row"),
        P("col", "row", None),
        P("col", None, "row"),
        P(None, None, "col"),
        P(None, "col", None),
        P(("row", "col"), None),
    )
    return jax.shard_map(
        local,
        mesh=mesh,
        in_specs=placed,
        out_specs=(P(("row", "col"), None, None), P("col", "row", None), P(None, "col", None)),
        check_vma=False,
    )
```

```python
import functools
import jax
import jax.numpy as jnp
from jax import lax
from jax.experimental import pallas as pl
from jax.experimental.pallas import tpu as pltpu
from jax.sharding import PartitionSpec as P

MESH = pl.DeviceIdType.MESH
NZ, NY, NX, NK = 8, 4, 4, 2
NC = NX * NK
W = 1024
SRC = 512
CH = W // NZ
CS = SRC // NY
CZ = CS // NZ
RB = 256
AHEAD = 3
ORDER = (4, 3, 5, 2, 6, 1, 7, 0)
F32 = jnp.float32
BF16 = jnp.bfloat16


def kernel(
    li, rhs, tiles, mi, mr, mt, ti, tr, tl,
    leaf_o, mid_o, top_o,
    liv, rv, tv, xv, usend, yrecv, up, down, rup, rdown, rbuf,
    mig, mtg, mrv, flag, flagr, tiv, trv, ybf,
    pbuf, p32, crecv, qbuf, xrecv, trt, tall, fall,
    load_sem, own_sem, y_s, y_r, mi_s, mi_r, mt_s, mt_r, mr_s, mr_r, fl_s, fl_r,
    up_s, up_r, dn_s, dn_r, r_s, f_s, r_r, c_s, c_r, x_s, x_r, t_s, t_r, a_s, a_r, mo_s, mo_r, to_s, to_r, ring_in,
):
    row = lax.axis_index("row")
    col = lax.axis_index("col")
    z, y = row // NY, row % NY
    x, k = col // NK, col % NK

    def at_y(other):
        return (z * NY + other, col)

    def at_z(other):
        return (other * NY + y, col)

    def at_c(other):
        return (row, other)

    def at_xz(other_x, other_z):
        return (other_z * NY + y, other_x * NK + k)

    def remote(src, dst, s, r, device):
        return pltpu.make_async_remote_copy(
            src_ref=src, dst_ref=dst, send_sem=s, recv_sem=r, device_id=device, device_id_type=MESH
        )

    y_peers = [(y + d) % NY for d in range(1, NY)]

    rbuf[...] = jnp.zeros_like(rbuf)
    barrier = pltpu.get_barrier_semaphore()
    for other in y_peers:
        pl.semaphore_signal(barrier, inc=1, device_id=at_y(other), device_id_type=MESH)
    for d in (1, NZ - 1):
        pl.semaphore_signal(barrier, inc=1, device_id=at_z((z + d) % NZ), device_id_type=MESH)
    for d in range(1, NC):
        pl.semaphore_signal(barrier, inc=1, device_id=at_c((col + d) % NC), device_id_type=MESH)

    loads = {}

    def load(name, src, dst):
        copy = pltpu.make_async_copy(src, dst, load_sem.at[len(loads)])
        copy.start()
        loads[name] = copy

    for i in range(W // RB):
        rows = slice(i * RB, (i + 1) * RB)
        load(f"r{i}", rhs.at[0, rows, :], rv.at[rows, :])
        load(f"l{i}", li.at[0, rows, : (i + 1) * RB], liv.at[rows, : (i + 1) * RB])
    for i in range(W // RB):
        rows = slice(i * RB, (i + 1) * RB)
        load(f"t{i}", tiles.at[0, rows, :], tv.at[rows, :])
    own_cols = pl.ds(pl.multiple_of(y * CS, CS), CS)
    own_rows = pl.ds(pl.multiple_of(y * 32, 32), 32)
    load("mi", mi, mig.at[y])
    load("mr", mr.at[:, :, own_cols], mrv.at[:, own_rows, :])
    load("mt", mt, mtg.at[y])
    load("ti", ti, tiv)
    load("tr", tr.at[:, :, own_cols], trv)

    flag[...] = jnp.full(flag.shape, tl[0, 0].astype(F32))

    for i in range(W // RB):
        rows = slice(i * RB, (i + 1) * RB)
        loads[f"r{i}"].wait()
        loads[f"l{i}"].wait()
        xv[rows, :] = jnp.dot(
            liv[rows, : (i + 1) * RB], rv[: (i + 1) * RB, :], preferred_element_type=F32
        ).astype(BF16)
    leaf_copy = pltpu.make_async_copy(xv, leaf_o.at[0], own_sem.at[0])
    leaf_copy.start()

    pl.semaphore_wait(barrier, NY + 2 + NC - 2)

    sends = []

    def start(copy):
        copy.start()
        sends.append(copy)
        return copy

    fl_copies, mr_copies = [], []
    for n, other in enumerate(y_peers):
        fl_copies.append(start(remote(flag, flagr.at[n], fl_s.at[n], fl_r.at[n], at_y(other))))
        cols = pl.ds(pl.multiple_of(other * CS, CS), CS)
        mr_copies.append(
            start(remote(mr.at[:, :, cols], mrv.at[:, own_rows, :], mr_s.at[n], mr_r.at[n], at_y(other)))
        )

    def mi_copy(n):
        return remote(mi, mig.at[y], mi_s.at[n], mi_r.at[n], at_y(y_peers[n]))

    def mt_copy(n):
        return remote(mt, mtg.at[y], mt_s.at[n], mt_r.at[n], at_y(y_peers[n]))

    def u_copy(j, n):
        return remote(
            usend.at[j, y_peers[n]], yrecv.at[n, j], y_s.at[n, j], y_r.at[n, j], at_y(y_peers[n])
        )

    for i in range(W // RB):
        loads[f"t{i}"].wait()
    for o in range(NZ):
        chunk_rows = pl.ds(pl.multiple_of((z + ORDER[o]) % NZ * CH, CH), CH)
        update = jnp.dot(tv[chunk_rows, :], xv[...], preferred_element_type=F32).astype(BF16)
        for s in range(NY):
            usend[o, s] = update[:, s * CS : (s + 1) * CS]
        if o < AHEAD:
            for n in (1, 0, 2):
                start(u_copy(o, n))

    above, below = at_z((z + 1) % NZ), at_z((z + NZ - 1) % NZ)

    def up_copy(step):
        part = pl.ds(0, 1 if step == 0 else 2)
        return remote(
            up.at[step, part], rup.at[step, part], up_s.at[step], up_r.at[step], above
        )

    def down_copy(step):
        part = pl.ds(1, 1) if step == 0 else pl.ds(0, 2)
        return remote(
            down.at[step, part], rdown.at[step, part], dn_s.at[step], dn_r.at[step], below
        )

    def r_copy(step):
        part = rbuf.at[:, pl.ds(pl.multiple_of(z * CH, CH), CH), :]
        return remote(part, part, r_s.at[step], r_r.at[z], at_z(z + step))

    def f_copy(step):
        part = rbuf.at[:, pl.ds(pl.multiple_of((z - 2) * CH, CH), CH), :]
        return remote(part, part, f_s.at[step], r_r.at[z - 2], at_z(z + step))

    def r_wait(other):
        part = rbuf.at[:, pl.ds(pl.multiple_of(other * CH, CH), CH), :]
        remote(part, part, r_s.at[0], r_r.at[other], at_z(other)).wait_recv()

    for copy in fl_copies:
        copy.wait_recv()
    loads["mr"].wait()
    for copy in mr_copies:
        copy.wait_recv()

    def summed(o):
        parts = [(usend[o, y].astype(F32), flag[0:1, :] > 0.5)]
        for n in range(NY - 1):
            u_copy(o, n).wait_recv()
            parts.append((yrecv[n, o].astype(F32), flagr[n, 0:1, :] > 0.5))
        if o + AHEAD < NZ:
            for n in (1, 0, 2):
                start(u_copy(o + AHEAD, n))
        one = sum(jnp.where(f, u, 0.0) for u, f in parts)
        zero = sum(jnp.where(f, 0.0, u) for u, f in parts)
        return zero, one

    zero, one = summed(0)
    up[0, 0] = zero.astype(BF16)
    down[0, 1] = one.astype(BF16)
    start(up_copy(0))
    start(down_copy(0))
    for step in range(1, NZ // 2):
        zero, one = summed(2 * step - 1)
        up_copy(step - 1).wait_recv()
        if step > 1:
            one += rup[step - 1, 1].astype(F32)
        up[step, 0] = (zero + rup[step - 1, 0].astype(F32)).astype(BF16)
        up[step, 1] = one.astype(BF16)
        start(up_copy(step))
        zero, one = summed(2 * step)
        down_copy(step - 1).wait_recv()
        if step > 1:
            zero += rdown[step - 1, 0].astype(F32)
        down[step, 0] = zero.astype(BF16)
        down[step, 1] = (one + rdown[step - 1, 1].astype(F32)).astype(BF16)
        start(down_copy(step))
    both = summed(NZ - 1)
    up_copy(NZ // 2 - 1).wait_recv()
    down_copy(NZ // 2 - 1).wait_recv()
    mine = pl.ds(pl.multiple_of(z * CH, CH), CH)
    for b in range(2):
        total = both[b] + rup[NZ // 2 - 1, b].astype(F32) + rdown[NZ // 2 - 1, b].astype(F32)
        rbuf[b, mine, :] = (mrv[b].astype(F32) - total).astype(BF16)
    for d in range(1, NX):
        pl.semaphore_signal(ring_in, inc=1, device_id=at_c((x + d) % NX * NK + k), device_id_type=MESH)

    for step in (2, 1, 7, 6, 5):

        @pl.when(z + step < NZ)
        def _():
            r_copy(step).start()

    for n in (1, 0, 2):
        start(mi_copy(n))
    for n in (1, 0, 2):
        start(mt_copy(n))

    @pl.when(z >= 2)
    def _():
        r_wait(z - 2)
        for step in (2, 1):

            @pl.when(z + step < NZ)
            def _():
                f_copy(step).start()

    loads["mi"].wait()
    for n in range(NY - 1):
        mi_copy(n).wait_recv()
    for other in range(NZ - 1):

        @pl.when((other < z) & (other != z - 2))
        def _():
            r_wait(other)

    turned = []
    for b in range(2):
        solved = jnp.dot(mig[:, b].reshape(CH, W), rbuf[b], preferred_element_type=F32)
        ybf[b] = solved.astype(BF16)
        turned.append(solved.T.astype(BF16))

    loads["mt"].wait()
    for n in range(NY - 1):
        mt_copy(n).wait_recv()
    core_copies = []
    for b in range(2):
        update = jnp.dot(turned[b], mtg[:, b].reshape(CH, W), preferred_element_type=F32)
        for c in range(NC):
            p32[c % NK, b, c // NK] = update[:, c * CH : (c + 1) * CH]
        pbuf[b] = p32[1 - k, b].astype(BF16)
        core_copies.append(
            start(remote(pbuf.at[b], crecv.at[b], c_s.at[b], c_r.at[b], at_c(x * NK + 1 - k)))
        )

    mid_copies = []
    for n, other in enumerate(y_peers):
        rows = pl.ds(pl.multiple_of(other * 32, 32), 32)
        mid_copies.append(start(remote(ybf.at[:, rows, :], mid_o.at[y], mo_s.at[n], mo_r.at[n], at_y(other))))
    mid_copy = pltpu.make_async_copy(ybf.at[:, own_rows, :], mid_o.at[y], own_sem.at[1])
    mid_copy.start()

    loads["tr"].wait()
    for b in range(2):
        trt[b] = trv[b].astype(F32).T

    for b in range(2):
        core_copies[b].wait_recv()
        for other in range(NX):
            part = (p32[k, b, other] + crecv[b, other].astype(F32)).astype(BF16)
            for slot in range(NZ):
                qbuf[other, slot, b] = part[slot * CZ : (slot + 1) * CZ, :]
    steps = [(dx, dz) for dz in (4, 3, 5, 2, 6, 1, 7, 0) for dx in (2, 1, 3, 0) if dx or dz]
    pl.semaphore_wait(ring_in, NX - 1)
    for dx, dz in steps:
        ox, oz = (x + dx) % NX, (z + dz) % NZ
        start(
            remote(qbuf.at[ox, oz], xrecv.at[x, z], x_s.at[dx, dz], x_r.at[x, z], at_xz(ox, oz))
        )
    total = qbuf[x, z].astype(F32)
    for dx, dz in reversed(steps):
        ox, oz = (x + dx) % NX, (z + dz) % NZ
        remote(
            xrecv.at[ox, oz], xrecv.at[ox, oz], x_s.at[dx, dz], x_r.at[ox, oz], at_xz(ox, oz)
        ).wait_recv()
        total += xrecv[ox, oz].astype(F32)
    my_cols = pl.ds(pl.multiple_of(z * CZ, CZ), CZ)

    tall[col] = (trt[:, my_cols, :] - total).astype(BF16)
    for d in range(1, NC):
        other = (col + d) % NC
        start(remote(tall.at[col], tall.at[col], t_s.at[d - 1], t_r.at[col], at_c(other)))
    loads["ti"].wait()
    for d in range(1, NC):
        other = (col + d) % NC
        remote(tall.at[other], tall.at[other], t_s.at[d - 1], t_r.at[other], at_c(other)).wait_recv()

    for b in range(2):
        resid = jnp.concatenate([tall[c, b] for c in range(NC)], axis=1)
        fall[z, b] = jnp.dot(resid, tiv[b], preferred_element_type=F32).astype(BF16)
    for d in range(1, NZ):
        other = (z + d) % NZ
        start(remote(fall.at[z], fall.at[z], a_s.at[d - 1], a_r.at[z], at_z(other)))
    outs = [leaf_copy, mid_copy]
    to_copies = []

    def pass_on(at, slot):
        for n in (1, 0, 2):
            to_copies.append(
                start(
                    remote(
                        fall.at[at], top_o.at[y, at], to_s.at[n, slot], to_r.at[n, at], at_y(y_peers[n])
                    )
                )
            )
        copy = pltpu.make_async_copy(fall.at[at], top_o.at[y, at], own_sem.at[2 + slot])
        copy.start()
        outs.append(copy)

    pass_on(z, 0)
    for slot, d in enumerate((1, 7, 2, 6, 3, 5, 4)):
        other = (z + d) % NZ
        remote(fall.at[other], fall.at[other], a_s.at[d - 1], a_r.at[other], at_z(other)).wait_recv()
        pass_on(other, slot + 1)

    for step in (7, 6, 5, 2, 1):

        @pl.when(z + step < NZ)
        def _():
            r_copy(step).wait_send()

    for step in (2, 1):

        @pl.when((z >= 2) & (z + step < NZ))
        def _():
            f_copy(step).wait_send()

    for copy in sends:
        copy.wait_send()
    for copy in outs:
        copy.wait()
    for n in range(NY - 1):
        mid_copies[n].wait_recv()
    for copy in to_copies:
        copy.wait_recv()


def hand_over(leaf, mid, top, leaf_o, mid_o, top_o, leaf_v, mid_v, raw_v, top_v, sem):
    rows = W // 4
    parts = [pl.ds(i * rows, rows) for i in range(4)]
    load_top = pltpu.make_async_copy(top, raw_v, sem.at[0, 0])
    load_mid = [
        pltpu.make_async_copy(mid.at[i], mid_v.at[:, :, i * CS : (i + 1) * CS], sem.at[0, 1 + i]) for i in range(NY)
    ]
    load_leaf = [
        pltpu.make_async_copy(leaf.at[0, part], leaf_v.at[part], sem.at[0, 1 + NY + i])
        for i, part in enumerate(parts)
    ]
    stores = [
        pltpu.make_async_copy(leaf_v.at[part], leaf_o.at[0, part], sem.at[1, i]) for i, part in enumerate(parts)
    ]
    store_mid = pltpu.make_async_copy(mid_v, mid_o, sem.at[1, 4])
    store_top = pltpu.make_async_copy(top_v, top_o, sem.at[1, 5])
    for copy in [load_top] + load_leaf + load_mid:
        copy.start()
    load_top.wait()
    for i in range(NY):
        for b in range(2):
            block = raw_v[i, :, b].reshape(CS, CH).astype(F32)
            top_v[b, :, i * CS : (i + 1) * CS] = block.T.astype(BF16)
    store_top.start()
    for load, store in zip(load_leaf, stores):
        load.wait()
        store.start()
    for copy in load_mid:
        copy.wait()
    store_mid.start()
    for copy in stores + [store_mid, store_top]:
        copy.wait()


def local(li, rhs, tiles, mi, mr, mt, ti, tr, tl):
    dma = pltpu.SemaphoreType.DMA
    vmem = pltpu.VMEM
    any_spec = pl.BlockSpec(memory_space=pl.ANY)
    n = NY - 1
    parts = pl.pallas_call(
        kernel,
        out_shape=(
            jax.ShapeDtypeStruct((1, W, SRC), BF16),
            jax.ShapeDtypeStruct((NY, 2, 32, CS), BF16),
            jax.ShapeDtypeStruct((NY, NZ, 2, CZ, CH), BF16),
        ),
        in_specs=[pl.BlockSpec(memory_space=pltpu.HBM)] * 8 + [pl.BlockSpec(memory_space=pltpu.SMEM)],
        out_specs=(any_spec,) * 3,
        scratch_shapes=[
            vmem((W, W), BF16),
            vmem((W, SRC), BF16),
            vmem((W, W), BF16),
            vmem((W, SRC), BF16),
            vmem((NZ, NY, CH, CS), BF16),
            vmem((n, NZ, CH, CS), BF16),
            vmem((NZ // 2, 2, CH, CS), BF16),
            vmem((NZ // 2, 2, CH, CS), BF16),
            vmem((NZ // 2, 2, CH, CS), BF16),
            vmem((NZ // 2, 2, CH, CS), BF16),
            vmem((2, W, CS), BF16),
            vmem((NY, 2, 32, W), BF16),
            vmem((NY, 2, 32, W), BF16),
            vmem((2, CH, CS), BF16),
            vmem((8, 128), F32),
            vmem((n, 8, 128), F32),
            vmem((2, W, CH), BF16),
            vmem((2, CH, CS), BF16),
            vmem((2, CH, CS), BF16),
            vmem((2, NX, CS, CH), BF16),
            vmem((NK, 2, NX, CS, CH), F32),
            vmem((2, NX, CS, CH), BF16),
            vmem((NX, NZ, 2, CZ, CH), BF16),
            vmem((NX, NZ, 2, CZ, CH), BF16),
            vmem((2, CS, CH), F32),
            vmem((NC, 2, CZ, CH), BF16),
            vmem((NZ, 2, CZ, CH), BF16),
            dma((17,)), dma((2 + NZ,)),
            dma((n, NZ)), dma((n, NZ)),
            dma((n,)), dma((n,)), dma((n,)), dma((n,)),
            dma((n,)), dma((n,)), dma((n,)), dma((n,)),
            dma((NZ // 2,)), dma((NZ // 2,)), dma((NZ // 2,)), dma((NZ // 2,)),
            dma((NZ,)), dma((3,)), dma((NZ,)),
            dma((2,)), dma((2,)), dma((NX, NZ)), dma((NX, NZ)),
            dma((NC - 1,)), dma((NC,)),
            dma((NZ - 1,)), dma((NZ,)),
            dma((n,)), dma((n,)), dma((n, NZ)), dma((n, NZ)),
            pltpu.SemaphoreType.REGULAR,
        ],
        compiler_params=pltpu.CompilerParams(
            collective_id=0, has_side_effects=True, vmem_limit_bytes=56 * 1024 * 1024
        ),
        cost_estimate=pl.CostEstimate(flops=2_700_000_000, bytes_accessed=8_000_000, transcendentals=0),
        name="forward_substitution",
    )(li, rhs, tiles, jnp.swapaxes(mi, 1, 2), mr, jnp.swapaxes(mt, 1, 2), ti, tr, tl)
    return pl.pallas_call(
        hand_over,
        out_shape=(
            jax.ShapeDtypeStruct((1, W, SRC), BF16),
            jax.ShapeDtypeStruct((2, 32, SRC), BF16),
            jax.ShapeDtypeStruct((2, CH, SRC), BF16),
        ),
        in_specs=[any_spec] * 3,
        out_specs=(any_spec,) * 3,
        scratch_shapes=[
            vmem((W, SRC), BF16),
            vmem((2, 32, SRC), BF16),
            vmem((NY, NZ, 2, CZ, CH), BF16),
            vmem((2, CH, SRC), BF16),
            dma((2, 9)),
        ],
        name="results",
    )(*parts)


def solution(mesh):
    placed = (
        P(("row", "col"), None, None),
        P(("row", "col"), None, None),
        P(("row", "col"), None, None),
        P("col", None, "row"),
        P("col", "row", None),
        P("col", None, "row"),
        P(None, None, "col"),
        P(None, "col", None),
        P(("row", "col"), None),
    )
    return jax.shard_map(
        local,
        mesh=mesh,
        in_specs=placed,
        out_specs=(P(("row", "col"), None, None), P("col", "row", None), P(None, "col", None)),
        check_vma=False,
    )
```
